256 devices in a mesh: grp: 8 (over x, core), dev: 32 (over z, y).
Axes of the slice: x: 4, y: 4, z: 8, core: 2. Of those that a mesh axis runs over, the one named last changes fastest.
Arguments:
- gap_field: float32 [1024, 768], P(('grp', 'dev')), may hold values from -6 to 6
- precond_weight: float32 [1024, 768], P(('grp', 'dev')), may hold values from 0.5 to 4
- slab_links: int32 [128, 4], P('dev'), may hold values from 0 to 127, as said below
- face_lengths: int32 [128, 4], P('dev'), may hold values from 64 to 128, as said below
- schur_inv: float32 [1024, 768, 768], P(('grp', 'dev')), may hold values from -40 to 40
- corner_map: int32 [1024, 24], P(('grp', 'dev')), may hold values from 0 to 3071
- corner_coupling: float32 [1024, 24, 768], P(('grp', 'dev')), may hold values from -0.21875 to 0.21875
- coarse_inv: float32 [3072, 3072], P('dev'), may hold values from -20 to 20, as said below
Outputs:
- multipliers: float32 [1024, 768], P(('grp', 'dev'))
- residual: float32 [1024, 768], P(('grp', 'dev'))
The draws below stay inside these ranges and needn't reach their ends.
Inputs may be any that keep to these rules, and one draw needn't show every extreme that they name: slab_links is a symmetric neighbour relation of a periodic two-dimensional grid of slab positions: position slab_links[p, 0] has p as its -a neighbour and slab_links[p, 1] has p as its +a neighbour (likewise columns 2 and 3 for b). Position p lies on device p // 4; the +a neighbours of all positions of one device lie on one other device, the -a neighbours on a third one, and the b neighbours on the device itself. `face_lengths`: the live length of a face equals that of the matching face across the interface; some face is fully live. coarse_inv is symmetric.
All inputs are finite; a program needn't handle non-finite values.
Results may differ from the reference program's by a relative error of at most 0.0003.
Values sent between devices are 32-bit elements; how exact they have to be, the bound alone decides.
A program may use at most 64 MiB of HBM per device.

```python
import math
import jax
import jax.numpy as jnp
from jax import lax

S_DEV = 4
FD = 128
KC = 24
NC = 3072
ITERS = 3
B = 768
NSLAB = 128
NS = 1024
N_GRP = 8


def slab_tables(key):
    base = jax.random.fold_in(key, 5)
    key_rows, key_slots, key_first, key_second = jax.random.split(base, 4)
    row_count = NSLAB // S_DEV
    row_device = jax.random.permutation(key_rows, row_count).astype(jnp.int32)
    scores = jax.random.randint(key_slots, (row_count, S_DEV), 0, 1 << 20) * S_DEV + jnp.arange(S_DEV, dtype=jnp.int32)[None, :]
    slot_order = jnp.argsort(scores, axis=1).astype(jnp.int32)
    position = row_device[:, None] * S_DEV + slot_order
    links_cell = jnp.stack([jnp.roll(position, -1, 0), jnp.roll(position, 1, 0), jnp.roll(position, -1, 1), jnp.roll(position, 1, 1)], axis=-1)
    length_first = jax.random.randint(key_first, (row_count, S_DEV), FD // 2, FD + 1).at[0, 0].set(FD)
    length_second = jax.random.randint(key_second, (row_count, S_DEV), FD // 2, FD + 1).at[0, 0].set(FD)
    lengths_cell = jnp.stack([length_first, jnp.roll(length_first, 1, 0), length_second, jnp.roll(length_second, 1, 1)], axis=-1)
    flat_position = position.reshape(-1)
    links = jnp.zeros((NSLAB, 4), jnp.int32).at[flat_position].set(links_cell.reshape(-1, 4).astype(jnp.int32))
    lengths = jnp.zeros((NSLAB, 4), jnp.int32).at[flat_position].set(lengths_cell.reshape(-1, 4).astype(jnp.int32))
    return (links, lengths)


def draw_slab_links(key, part):
    return slab_tables(key)[0]


def draw_face_lengths(key, part):
    return slab_tables(key)[1]


def symmetric_body(key, count, width, diagonal, top_scale):
    key_raw, key_scale = jax.random.split(key)
    raw = jnp.clip(jax.random.normal(key_raw, (count, width, width), jnp.float32), -6.0, 6.0)
    scales = jnp.exp(jax.random.uniform(key_scale, (count, width), jnp.float32, 0.0, math.log(top_scale)))
    symmetric = (raw + jnp.swapaxes(raw, 1, 2)) * (0.5 / math.sqrt(2.0 * width))
    identity = (jnp.arange(width)[:, None] == jnp.arange(width)[None, :]).astype(jnp.float32)
    core = symmetric * (1.0 - identity) + diagonal * identity
    roots = jnp.sqrt(scales)
    return core * roots[:, :, None] * roots[:, None, :]


def draw_schur_inv(key, part):
    return symmetric_body(jax.random.fold_in(key, 11), NS, B, 2.5, 10.0)


def draw_coarse_inv(key, part):
    return symmetric_body(jax.random.fold_in(key, 13), 1, NC, 3.0, 4.0)[0]


def plant(entries, rng, low, largest):
    extent = entries.shape
    index_at = [jax.random.randint(jax.random.fold_in(rng, axis), (), 0, extent[axis]) for axis in range(len(extent))]
    entries = entries.at[tuple(index_at)].set(low)
    longest = extent.index(max(extent))
    index_at[longest] = (index_at[longest] + 1) % extent[longest]
    return entries.at[tuple(index_at)].set(largest)


def level_of(rng, shape, cuts, least, largest):
    loudness = 1.0
    for axis_at, parts in cuts:
        heights = jax.random.uniform(jax.random.fold_in(jax.random.fold_in(rng, 6), axis_at), (parts,), jnp.float32, least / len(cuts), largest / len(cuts))
        loudness = loudness * jnp.repeat(jnp.exp(heights), shape[axis_at] // parts).reshape((-1,) + (1,) * (len(shape) - 1 - axis_at))
    return loudness


def centred(own_key, dims, scale, bound, cuts=(), held_as=jnp.bfloat16):
    result = jax.random.normal(own_key, dims, jnp.float32) * scale
    if len(cuts) > 0:
        result = level_of(own_key, dims, cuts, -0.22, 0.18) * result
    return jnp.clip(result, min=-bound, max=bound).astype(held_as)


def setup_inputs(seed: int = 0) -> dict:
    streams_of = jax.random.split(jax.random.key(seed), 9)
    gap_field = centred(streams_of[0], (NS, B), 1.0, 6.0, ((0, 256),), jnp.float32)
    precond_weight = jnp.clip(jnp.exp(math.log(4.0) - 2.0794415 * jax.random.uniform(streams_of[1], (NS, B), jnp.float32) ** level_of(streams_of[1], (NS, B), ((0, 256),), -0.2, 0.2)), 0.5, 4.0)
    slab_links = draw_slab_links(jax.random.fold_in(streams_of[8], 71), 0)
    face_lengths = draw_face_lengths(jax.random.fold_in(streams_of[8], 71), 0)
    schur_inv = draw_schur_inv(jax.random.fold_in(streams_of[8], 71), 0)
    corner_map = plant(jax.random.randint(streams_of[5], (NS, KC), 0, NC), jax.random.fold_in(streams_of[5], 1), 0, NC - 1).astype(jnp.int32)
    corner_coupling = centred(streams_of[6], (NS, KC, B), B ** -0.5, 0.21875, ((0, 256),), jnp.float32)
    coarse_inv = draw_coarse_inv(jax.random.fold_in(streams_of[8], 71), 0)
    return {"gap_field": gap_field, "precond_weight": precond_weight, "slab_links": slab_links, "face_lengths": face_lengths, "schur_inv": schur_inv, "corner_map": corner_map, "corner_coupling": corner_coupling, "coarse_inv": coarse_inv}


highest = lax.Precision.HIGHEST


def reference(gap_field, precond_weight, slab_links, face_lengths, schur_inv, corner_map, corner_coupling, coarse_inv):
    face_sign = jnp.array([1.0, -1.0, 1.0, -1.0, 1.0, -1.0], jnp.float32)[:, None]
    live_slab = (jnp.arange(FD, dtype=jnp.int32)[None, None, :] < face_lengths[:, :, None]).astype(jnp.float32)
    slab_mask = jnp.concatenate([jnp.ones((NSLAB, 2, FD), jnp.float32), live_slab], axis=1)
    face_mask = jnp.broadcast_to(slab_mask[None], (N_GRP, NSLAB, 6, FD)).reshape(NS, 6, FD)

    def opposite(values):
        grouped = values.reshape(N_GRP, NSLAB, 6, FD)
        pieces = [jnp.roll(grouped[:, :, 1], -1, 0), jnp.roll(grouped[:, :, 0], 1, 0),
                  grouped[:, slab_links[:, 0], 3], grouped[:, slab_links[:, 1], 2],
                  grouped[:, slab_links[:, 2], 5], grouped[:, slab_links[:, 3], 4]]
        return jnp.stack(pieces, axis=2).reshape(NS, 6, FD)

    def interface_jump(values):
        return face_mask * face_sign * (values - opposite(values))

    def operator(direction):
        face_load = (face_sign * direction).reshape(NS, B)
        response = jnp.einsum("sij,sj->si", schur_inv, face_load, precision=highest)
        corner_load = jnp.einsum("skj,sj->sk", corner_coupling, face_load, precision=highest)
        coarse_rhs = jnp.zeros((NC,), jnp.float32).at[corner_map.reshape(-1)].add(corner_load.reshape(-1))
        coarse_sol = jnp.dot(coarse_inv, coarse_rhs, precision=highest)
        response = response + jnp.einsum("skj,sk->sj", corner_coupling, coarse_sol[corner_map], precision=highest)
        return interface_jump(response.reshape(NS, 6, FD))

    def inner(first, second):
        return 0.5 * jnp.sum(first * second)

    weights = precond_weight.reshape(NS, 6, FD)
    scaling = weights + opposite(weights)
    residual = interface_jump(gap_field.reshape(NS, 6, FD))
    scaled = scaling * residual
    direction = scaled
    norm_now = inner(residual, scaled)
    solution = jnp.zeros_like(residual)
    for iteration in range(ITERS):
        image = operator(direction)
        step_size = norm_now / inner(direction, image)
        solution = solution + step_size * direction
        residual = residual - step_size * image
        if iteration + 1 < ITERS:
            scaled = scaling * residual
            norm_next = inner(residual, scaled)
            direction = scaled + (norm_next / norm_now) * direction
            norm_now = norm_next
    return solution.reshape(NS, B), residual.reshape(NS, B)
```

```python
import functools

import jax
import jax.numpy as jnp
from jax import lax
from jax.experimental import pallas as pl
from jax.experimental.pallas import tpu as pltpu
from jax.sharding import PartitionSpec as P

ITERS = 3
MESH = pl.DeviceIdType.MESH
F32 = jnp.float32
BF16 = jnp.bfloat16
N_GRP, N_DEV = 8, 32
SUB, KC, FD, FACES = 4, 24, 128, 6
ROWS = SUB * FACES
CK = SUB * KC
HI, LO = 32, 96
PIECES = 2 * CK // 8


def iota(shape, dim):
    return lax.broadcasted_iota(jnp.int32, shape, dim)


def split(x, parts):
    out = []
    for _ in range(parts - 1):
        top = x.astype(BF16)
        out.append(top)
        x = x - top.astype(F32)
    out.append(x.astype(BF16))
    return out


def dot(a, b):
    return jnp.dot(a, b, preferred_element_type=F32)


def dot_nt(a, b):
    return lax.dot_general(a, b, (((1,), (1,)), ((), ())), preferred_element_type=F32)


def pick_rows(one_hot, x):
    return sum(dot(one_hot, part) for part in split(x, 3))


def lane_sums(x):
    ones = jnp.ones((8, x.shape[1]), BF16)
    return sum(dot_nt(ones, part) for part in split(x, 3))[0:1]


def total(x):
    return jnp.sum(jnp.sum(x, axis=0, keepdims=True), axis=1, keepdims=True)


def await_bytes(ref, sem):
    pltpu.make_async_copy(ref, ref, sem).wait()


def kernel(
    gap_hbm, wgt_hbm, links_hbm, lens_hbm, schur_hbm, map_hbm, coup_hbm, coarse_hbm,
    x_out, r_out,
    gap_v, wgt_v, links_v, lens_v, map_v, schur_v, coup_v, coarse_v, coarse_p,
    fields0, sent0, fields, sent, target, sign_mask, tmp, tmp2,
    meta, tiles_a, tiles_b, coup_a, coup_x, own_w, next_w,
    high_mask, low_hot, gather_hi, gather_lo, acc_v, coarse_b,
    round1, round2, round3,
    local_sem, send_sem, recv_sem,
):
    g, d = lax.axis_index("grp"), lax.axis_index("dev")
    lane = iota((8, FD), 1)
    lane1 = iota((1, FD), 1)

    loads = [
        pltpu.make_async_copy(gap_hbm, gap_v, local_sem.at[0]),
        pltpu.make_async_copy(wgt_hbm, wgt_v, local_sem.at[1]),
        pltpu.make_async_copy(links_hbm, links_v, local_sem.at[2]),
        pltpu.make_async_copy(lens_hbm, lens_v, local_sem.at[3]),
        pltpu.make_async_copy(map_hbm, map_v, local_sem.at[4]),
    ]
    loads += [
        pltpu.make_async_copy(coup_hbm.at[s], coup_v.at[pl.ds(KC * s, KC), :], local_sem.at[5 + s])
        for s in range(SUB)
    ]
    loads.append(pltpu.make_async_copy(coarse_hbm, coarse_v, local_sem.at[9]))
    loads += [
        pltpu.make_async_copy(
            schur_hbm.at[s], schur_v.at[pl.ds(768 * s, 768), :], local_sem.at[10 + s]
        )
        for s in range(SUB)
    ]

    barrier = pltpu.get_barrier_semaphore()

    def greet(axis, n):
        def body(k, c):
            t = lax.rem(lax.axis_index(axis) + k, n)
            pl.semaphore_signal(barrier, inc=1, device_id={axis: t}, device_id_type=MESH)
            return c

        lax.fori_loop(1, n, body, 0)

    own_rows = pl.ds(pl.multiple_of(4 * d, 4), 4)
    for buf in [fields0.at[i] for i in range(2)] + [fields.at[i] for i in range(ITERS)]:
        buf[own_rows, :] = jnp.zeros((4, FD), F32)
        buf[160:256, :] = jnp.zeros((96, FD), F32)
    meta[32:128, :] = jnp.zeros((96, FD), F32)
    greet("dev", N_DEV)
    greet("grp", N_GRP)
    for load in loads:
        load.start()

    def send(src, dst, sem, axis, t):
        pltpu.make_async_remote_copy(
            src_ref=src, dst_ref=dst, send_sem=send_sem.at[sem], recv_sem=recv_sem.at[sem],
            device_id={axis: t}, device_id_type=MESH,
        ).start()

    def send_all(axis, n, src_of, dst, sem):
        def body(k, c):
            t = lax.rem(lax.axis_index(axis) + k, n)
            send(src_of(t), dst, sem, axis, t)
            return c

        lax.fori_loop(1, n, body, 0)

    acc_v[...] = jnp.zeros_like(acc_v)
    tmp[...] = jnp.zeros_like(tmp)
    tmp2[...] = jnp.zeros_like(tmp2)

    for load in loads[:5]:
        load.wait()
    links = links_v[...].astype(F32)
    tmp[0:SUB, 0:KC] = map_v[...].astype(F32)
    tmp2[0:SUB, 0:4] = links
    map_rows, link_rows = tmp[...], tmp2[...]
    meta_row = jnp.zeros((1, FD), F32)
    for s in range(SUB):
        meta_row += pltpu.roll(map_rows, KC * s, 1)[s : s + 1] if s else map_rows[0:1]
        meta_row += pltpu.roll(link_rows, CK + 4 * s, 1)[s : s + 1]
    meta[pl.ds(d, 1), :] = meta_row

    plus_dev = jnp.floor(links[0:1, 0:1] * 0.25)
    to_plus = (iota((N_DEV * SUB, FD), 0) // SUB).astype(F32) == plus_dev

    def chosen(values):
        first = jnp.concatenate([values[8:12]] * 32, axis=0)
        second = jnp.concatenate([values[12:16]] * 32, axis=0)
        return jnp.where(to_plus, first, second)

    own0 = []
    for i, src in enumerate((gap_v, wgt_v)):
        for f in range(FACES):
            fields0[i, 128 + 4 * f : 132 + 4 * f, :] = src[:, FD * f : FD * (f + 1)]
        values = fields0[i, 128:152, :]
        own0.append(values)
        sent0[i] = chosen(values)

    up, down = lax.rem(g + 1, N_GRP), lax.rem(g + N_GRP - 1, N_GRP)
    pl.semaphore_wait(barrier, N_DEV + N_GRP - 2)

    def send_fields(buf, out, sem):
        send_all(
            "dev", N_DEV,
            lambda t: out.at[pl.ds(pl.multiple_of(4 * t, 4), 4), :],
            buf.at[pl.ds(pl.multiple_of(4 * d, 4), 4), :], sem,
        )
        send(buf.at[pl.ds(132, 4), :], buf.at[pl.ds(152, 4), :], sem, "grp", down)
        send(buf.at[pl.ds(128, 4), :], buf.at[pl.ds(156, 4), :], sem, "grp", up)

    def await_fields(buf, sems, sem):
        await_bytes(buf.at[pl.ds(0, 4 * (N_DEV + 1)), :], sems.at[sem])

    S_F0, S_META, S_TA, S_TB, S_CX, S_F, S_R1, S_R2, S_R3 = 0, 2, 3, 4, 5, 6, 9, 12, 15

    for i in range(2):
        send_fields(fields0.at[i], sent0.at[i], S_F0 + i)
    own_meta = meta.at[pl.ds(d, 1), :]
    send_all("dev", N_DEV, lambda t: own_meta, own_meta, S_META)
    send(own_meta, meta.at[pl.ds(32, 1), :], S_META, "grp", down)
    send(own_meta, meta.at[pl.ds(33, 1), :], S_META, "grp", up)
    for load in loads[5:9]:
        load.wait()
    for j in range(PIECES):
        @pl.when(d != j)
        def _():
            send(
                coup_v.at[pl.ds(8 * (j % 12), 8), pl.ds(FD * (2 + j // 12), FD)],
                tiles_a.at[pl.ds(pl.multiple_of(8 * d, 8), 8), :], S_TA, "dev", j,
            )
    send(coup_v.at[:, pl.ds(FD, FD)], coup_x.at[0], S_CX, "grp", down)
    send(coup_v.at[:, pl.ds(0, FD)], coup_x.at[1], S_CX, "grp", up)

    row24 = iota((ROWS, FD), 0)
    sign = (1 - 2 * (lax.rem(row24 // 4, 2))).astype(F32)
    sign_mask[0:8, :] = sign[0:8]
    lens = lens_v[...]
    for k in range(4):
        live = iota((SUB, FD), 1) < lens[:, k : k + 1]
        sign_mask[8 + 4 * k : 12 + 4 * k, :] = jnp.where(live, 1.0 - 2.0 * (k % 2), 0.0)
    jump_sign = sign_mask[...]
    slot = iota((SUB, FD), 0).astype(F32)
    slot_of = links - 4.0 * jnp.floor(links * 0.25)
    ones4 = jnp.ones((SUB, FD), F32)
    target[0:4, :] = slot + 152.0
    target[4:8, :] = slot + 156.0
    target[8:12, :] = ones4 * links[:, 0:1]
    target[12:16, :] = ones4 * links[:, 1:2]
    target[16:20, :] = ones4 * (slot_of[:, 2:3] + 148.0)
    target[20:24, :] = ones4 * (slot_of[:, 3:4] + 144.0)
    targets = jnp.concatenate([target[...]] * 2, axis=1)
    opposite_hot = (targets == iota((ROWS, 256), 1).astype(F32)).astype(BF16)

    loads[9].wait()
    coarse_p[...] = jnp.zeros_like(coarse_p)
    for j in range(HI):
        coarse_p[:, FD * j : FD * j + LO] = coarse_v[:, LO * j : LO * (j + 1)]
    for f in range(FACES):
        for s in range(SUB):
            r = f * SUB + s
            own_w[f, KC * s : KC * (s + 1), :] = (
                coup_v[KC * s : KC * (s + 1), FD * f : FD * (f + 1)] * jump_sign[r : r + 1]
            )

    for i in range(2):
        await_fields(fields0.at[i], recv_sem, S_F0 + i)
    residual = jump_sign * (own0[0] - pick_rows(opposite_hot, fields0[0]))
    scaling = own0[1] + pick_rows(opposite_hot, fields0[1])
    scaled = scaling * residual
    result = jnp.zeros_like(residual)
    direction = image_dir = local_dir = None
    coarse_dir = norm_before = curve_before = None

    for it in range(ITERS):
        load_now = sign * scaled
        for s in range(SUB):
            part = jnp.zeros((KC, FD), F32)
            for f in range(FACES):
                r = f * SUB + s
                part += coup_v[KC * s : KC * (s + 1), FD * f : FD * (f + 1)] * load_now[r : r + 1]
            acc_v[KC * s : KC * (s + 1), :] = part
        r1, r2, r3 = round1.at[it], round2.at[it], round3.at[it]
        r1[pl.ds(d, 1), :] = lane_sums(acc_v[...])
        own = r1.at[pl.ds(d, 1), :]
        send_all("dev", N_DEV, lambda t: own, own, S_R1 + it)

        if it == 0:
            for load in loads[10:]:
                load.wait()
        response = jnp.zeros((ROWS, FD), F32)
        for s in range(SUB):
            def block(f, out):
                rows = pl.ds(pl.multiple_of(768 * s + FD * f, FD), FD)
                part = jnp.zeros((FD, FD), F32)
                for h in range(FACES):
                    r = h * SUB + s
                    part += schur_v[rows, FD * h : FD * (h + 1)] * load_now[r : r + 1]
                put = jnp.where(row24 == f * SUB + s, 1.0, 0.0).astype(BF16)
                for piece in split(part, 3):
                    out += dot_nt(put, piece)
                return out

            response = lax.fori_loop(0, FACES, block, response)
        buf, out = fields.at[it], sent.at[it]
        buf[128:152, :] = response
        out[...] = chosen(response)
        send_fields(buf, out, S_F + it)
        norm_part = 0.5 * total(residual * scaled)
        curve_part = total(load_now * response)
        cross_part = None
        if it:
            cross_part = total(load_now * local_dir + sign * direction * response)

        if it == 0:
            await_bytes(meta.at[pl.ds(0, N_DEV + 1), :], recv_sem.at[S_META])
            table = meta[...]
            high = jnp.floor((table + 0.5) * (1.0 / LO))
            low = table - LO * high
            hi_rows = iota((HI, FD), 0).astype(F32)
            lo_rows = iota((FD, FD), 0).astype(F32)
            for j in range(N_DEV):
                cols = slice(FD * j, FD * (j + 1))
                high_mask[:, cols] = jnp.where(hi_rows == high[j : j + 1], 1.0, 0.0)
                low_hot[:, cols] = jnp.where(lo_rows == low[j : j + 1], 1.0, 0.0).astype(BF16)

            @pl.when(d < PIECES)
            def _():
                tiles_a[pl.ds(pl.multiple_of(8 * d, 8), 8), :] = coup_v[
                    pl.ds(pl.multiple_of(8 * lax.rem(d, 12), 8), 8),
                    pl.ds(pl.multiple_of(FD * (2 + d // 12), FD), FD),
                ]
                await_bytes(tiles_a.at[pl.ds(0, 8 * (N_DEV - 1)), :], recv_sem.at[S_TA])
                spread = jnp.where(
                    iota((256, FD), 0) // 8 == iota((256, FD), 1), 1.0, 0.0
                ).astype(BF16)
                wanted = dot(spread, table.astype(BF16))
                which = CK + 1 - d // 12
                source = jnp.sum(
                    jnp.where(iota((256, FD), 1) == which, wanted, 0.0), axis=1, keepdims=True
                )
                source = 8.0 * jnp.floor(source * 0.25) + lax.rem(
                    iota((256, 1), 0), 8
                ).astype(F32)
                hot = jnp.where(iota((256, 256), 1).astype(F32) == source, 1.0, 0.0).astype(BF16)
                tiles_b[...] = pick_rows(hot, tiles_a[...])
                here = pl.ds(pl.multiple_of(8 * d, 8), 8)
                coup_a[here, :] = tiles_b[here, :]
                send_all(
                    "dev", N_DEV,
                    lambda t: tiles_b.at[pl.ds(pl.multiple_of(8 * t, 8), 8), :],
                    coup_a.at[here, :], S_TB,
                )

        await_bytes(r1.at[pl.ds(0, N_DEV - 1), :], recv_sem.at[S_R1 + it])
        corner = r1[...]
        top = corner.astype(BF16).astype(F32)
        rest = corner - top
        summed = jnp.zeros((2 * HI, FD), F32)
        for c in range(N_DEV // 2):
            pieces = []
            for source in (top, rest):
                pieces.append(
                    jnp.concatenate(
                        [
                            high_mask[:, FD * j : FD * (j + 1)] * source[j : j + 1]
                            for j in (2 * c, 2 * c + 1)
                        ],
                        axis=1,
                    )
                )
            both = jnp.concatenate(pieces, axis=0).astype(BF16)
            summed += dot_nt(both, low_hot[:, 256 * c : 256 * (c + 1)])
        slab_rhs = summed[0:HI] + summed[HI:]
        coarse_b[...] = slab_rhs
        part = jnp.zeros((CK, FD), F32)
        for j in range(HI):
            part += coarse_p[:, FD * j : FD * (j + 1)] * slab_rhs[j : j + 1]
        acc_v[0:CK, :] = part
        row = lane_sums(acc_v[...])
        row = jnp.where(lane1 == LO, norm_part, row)
        row = jnp.where(lane1 == LO + 1, curve_part, row)
        if it:
            row = jnp.where(lane1 == LO + 2, cross_part, row)
        r2[pl.ds(2 * g, 1), :] = row
        r2[pl.ds(2 * g + 1, 1), :] = coarse_b[pl.ds(d, 1), :]
        mine = r2.at[pl.ds(pl.multiple_of(2 * g, 2), 2), :]
        send_all("grp", N_GRP, lambda t: mine, mine, S_R2 + it)

        if it == 0:
            columns = table.T[0:CK]
            lane_f = iota((CK, FD), 1).astype(F32)

            def column(device):
                return jnp.sum(jnp.where(lane_f == device, columns, 0.0), axis=1, keepdims=True)

            def permuted(values, k):
                groups = []
                for s in range(SUB):
                    got = jnp.zeros((KC, FD), F32)
                    for j in range(SUB):
                        same = slot_of[s : s + 1, k : k + 1] == float(j)
                        got = jnp.where(same, values[KC * j : KC * (j + 1)], got)
                    groups.append(got)
                return jnp.concatenate(groups, axis=0)

            wide = jnp.zeros((CK, FD), F32)
            own_map = column(d.astype(F32)) + wide
            minus_dev = jnp.floor(links[0:1, 1:2] * 0.25)
            maps = [
                own_map,
                column(32.0) + wide,
                column(33.0) + wide,
                permuted(column(plus_dev) + wide, 0),
                permuted(column(minus_dev) + wide, 1),
                permuted(own_map, 2),
                permuted(own_map, 3),
            ]
            for i, m in enumerate(maps):
                high = jnp.floor((m + 0.5) * (1.0 / LO))
                rows = slice(CK * i, CK * (i + 1))
                gather_hi[rows, :] = jnp.where(high == lane_f, 1.0, 0.0).astype(BF16)
                gather_lo[rows, :] = jnp.where(m - LO * high == lane_f, 1.0, 0.0)

        await_bytes(r2.at[pl.ds(0, 2 * (N_GRP - 1)), :], recv_sem.at[S_R2 + it])
        pairs = r2[...]
        even = lax.rem(iota((2 * N_GRP, FD), 0), 2) == 0
        sol_row = jnp.sum(jnp.where(even, pairs, 0.0), axis=0, keepdims=True)
        rhs_row = jnp.sum(jnp.where(even, 0.0, pairs), axis=0, keepdims=True)
        row = jnp.where(
            lane1 == LO + 3, jnp.sum(sol_row * rhs_row, axis=1, keepdims=True), sol_row
        )
        if it:
            row = jnp.where(
                lane1 == LO + 4, jnp.sum(sol_row * coarse_dir, axis=1, keepdims=True), row
            )
        r3[pl.ds(d, 1), :] = row
        own3 = r3.at[pl.ds(d, 1), :]
        send_all("dev", N_DEV, lambda t: own3, own3, S_R3 + it)

        await_fields(buf, recv_sem, S_F + it)
        local_jump = jump_sign * (response - pick_rows(opposite_hot, buf[...]))
        if it == 0:
            @pl.when(d < PIECES)
            def _():
                await_bytes(coup_a.at[pl.ds(0, 8 * (PIECES - 1)), :], recv_sem.at[S_TB])

            @pl.when(d >= PIECES)
            def _():
                await_bytes(coup_a.at[pl.ds(0, 8 * PIECES), :], recv_sem.at[S_TB])

            await_bytes(coup_x, recv_sem.at[S_CX])
            beyond = [
                coup_x[0],
                coup_x[1],
                permuted(coup_a[CK : 2 * CK, :], 0),
                permuted(coup_a[0:CK, :], 1),
                permuted(coup_v[:, FD * 5 : FD * 6], 2),
                permuted(coup_v[:, FD * 4 : FD * 5], 3),
            ]
            for f in range(FACES):
                for s in range(SUB):
                    r = f * SUB + s
                    next_w[f, KC * s : KC * (s + 1), :] = (
                        -jump_sign[r : r + 1] * beyond[f][KC * s : KC * (s + 1)]
                    )

        await_bytes(r3.at[pl.ds(0, N_DEV - 1), :], recv_sem.at[S_R3 + it])
        coarse_sol = r3[...]
        sums = jnp.sum(coarse_sol, axis=0, keepdims=True)
        norm_now = sums[:, LO : LO + 1]
        curve = sums[:, LO + 1 : LO + 2] + sums[:, LO + 3 : LO + 4]
        padded = jnp.concatenate([coarse_sol, jnp.zeros((FD - HI, FD), F32)], axis=0)
        at_corner = []
        sol_parts = split(padded, 3)
        for i in range(7):
            rows = slice(CK * i, CK * (i + 1))
            hot = gather_hi[rows, :]
            got = sum(dot(hot, p) for p in sol_parts) * gather_lo[rows, :]
            at_corner.append(jnp.sum(got, axis=1, keepdims=True))
        for f in range(FACES):
            both = own_w[f] * at_corner[0] + next_w[f] * at_corner[1 + f]
            for s in range(SUB):
                r = f * SUB + s
                target[r : r + 1, :] = jnp.sum(
                    both[KC * s : KC * (s + 1)], axis=0, keepdims=True
                )
        image = local_jump + target[...]

        if it == 0:
            direction, image_dir, local_dir, coarse_dir = scaled, image, response, rhs_row
        else:
            ratio = norm_now / norm_before
            cross = sums[:, LO + 2 : LO + 3] + 2.0 * sums[:, LO + 4 : LO + 5]
            curve = curve + ratio * cross + ratio * ratio * curve_before
            direction = scaled + ratio * direction
            image_dir = image + ratio * image_dir
            local_dir = response + ratio * local_dir
            coarse_dir = rhs_row + ratio * coarse_dir
        step = norm_now / curve
        norm_before, curve_before = norm_now, curve
        result = result + step * direction
        residual = residual - step * image_dir
        scaled = scaling * residual

    for f in range(FACES):
        x_out[:, FD * f : FD * (f + 1)] = result[4 * f : 4 * f + 4]
        r_out[:, FD * f : FD * (f + 1)] = residual[4 * f : 4 * f + 4]

    for i in range(2):
        await_fields(fields0.at[i], send_sem, S_F0 + i)
    await_bytes(meta.at[pl.ds(0, N_DEV + 1), :], send_sem.at[S_META])

    @pl.when(d < PIECES)
    def _():
        await_bytes(tiles_a.at[pl.ds(0, 8 * (PIECES - 1)), :], send_sem.at[S_TA])
        await_bytes(tiles_b.at[pl.ds(0, 8 * (N_DEV - 1)), :], send_sem.at[S_TB])

    @pl.when(d >= PIECES)
    def _():
        await_bytes(tiles_a.at[pl.ds(0, 8 * PIECES), :], send_sem.at[S_TA])

    await_bytes(coup_x, send_sem.at[S_CX])
    for it in range(ITERS):
        await_fields(fields.at[it], send_sem, S_F + it)
        await_bytes(round1.at[it].at[pl.ds(0, N_DEV - 1), :], send_sem.at[S_R1 + it])
        await_bytes(round2.at[it].at[pl.ds(0, 2 * (N_GRP - 1)), :], send_sem.at[S_R2 + it])
        await_bytes(round3.at[it].at[pl.ds(0, N_DEV - 1), :], send_sem.at[S_R3 + it])


def per_device(*args):
    vmem = lambda *shape: pltpu.VMEM(shape, F32)
    field = jax.ShapeDtypeStruct((SUB, FACES * FD), F32)
    return pl.pallas_call(
        kernel,
        out_shape=(field, field),
        in_specs=[pl.BlockSpec(memory_space=pl.ANY)] * 8,
        out_specs=(pl.BlockSpec(memory_space=pltpu.VMEM),) * 2,
        scratch_shapes=[
            vmem(SUB, 768), vmem(SUB, 768),
            pltpu.VMEM((SUB, 4), jnp.int32), pltpu.VMEM((SUB, 4), jnp.int32),
            pltpu.VMEM((SUB, KC), jnp.int32),
            vmem(SUB * 768, 768), vmem(CK, 768), vmem(CK, 3072), vmem(CK, HI * FD),
            vmem(2, 256, FD), vmem(2, 128, FD),
            vmem(ITERS, 256, FD), vmem(ITERS, 128, FD),
            vmem(ROWS, FD), vmem(ROWS, FD), vmem(8, FD), vmem(8, FD),
            vmem(FD, FD), vmem(256, FD), vmem(256, FD), vmem(2 * CK, FD), vmem(2, CK, FD),
            vmem(FACES, CK, FD), vmem(FACES, CK, FD),
            vmem(HI, HI * FD), pltpu.VMEM((FD, HI * FD), BF16),
            pltpu.VMEM((7 * CK, FD), BF16), vmem(7 * CK, FD), vmem(FD, FD), vmem(HI, FD),
            vmem(ITERS, N_DEV, FD), vmem(ITERS, 2 * N_GRP, FD), vmem(ITERS, N_DEV, FD),
            pltpu.SemaphoreType.DMA((14,)),
            pltpu.SemaphoreType.DMA((18,)),
            pltpu.SemaphoreType.DMA((18,)),
        ],
        compiler_params=pltpu.CompilerParams(
            collective_id=0, has_side_effects=True, vmem_limit_bytes=48 * 1024 * 1024
        ),
    )(*args)


def solution(mesh):
    return jax.shard_map(
        per_device,
        mesh=mesh,
        in_specs=(
            P(("grp", "dev"), None),
            P(("grp", "dev"), None),
            P("dev", None),
            P("dev", None),
            P(("grp", "dev"), None, None),
            P(("grp", "dev"), None),
            P(("grp", "dev"), None, None),
            P("dev", None),
        ),
        out_specs=(P(("grp", "dev"), None), P(("grp", "dev"), None)),
        check_vma=False,
    )
```

```python
import functools

import jax
import jax.numpy as jnp
from jax import lax
from jax.experimental import pallas as pl
from jax.experimental.pallas import tpu as pltpu
from jax.sharding import PartitionSpec as P

ITERS = 3
MESH = pl.DeviceIdType.MESH
F32 = jnp.float32
BF16 = jnp.bfloat16
N_GRP, N_DEV = 8, 32
SUB, KC, FD, FACES = 4, 24, 128, 6
ROWS = SUB * FACES
CK = SUB * KC
HI, LO = 32, 96
PIECES = 2 * CK // 8


def iota(shape, dim):
    return lax.broadcasted_iota(jnp.int32, shape, dim)


def split(x, parts):
    out = []
    for _ in range(parts - 1):
        top = x.astype(BF16)
        out.append(top)
        x = x - top.astype(F32)
    out.append(x.astype(BF16))
    return out


def dot(a, b):
    return jnp.dot(a, b, preferred_element_type=F32)


def dot_nt(a, b):
    return lax.dot_general(a, b, (((1,), (1,)), ((), ())), preferred_element_type=F32)


def pick_rows(one_hot, x):
    return sum(dot(one_hot, part) for part in split(x, 3))


def lane_sums(x):
    ones = jnp.ones((8, x.shape[1]), BF16)
    return sum(dot_nt(ones, part) for part in split(x, 3))[0:1]


def total(x):
    return jnp.sum(jnp.sum(x, axis=0, keepdims=True), axis=1, keepdims=True)


def await_bytes(ref, sem):
    pltpu.make_async_copy(ref, ref, sem).wait()


def kernel(
    gap_hbm, wgt_hbm, links_hbm, lens_hbm, schur_hbm, map_hbm, coup_hbm, coarse_hbm,
    x_out, r_out,
    gap_v, wgt_v, links_v, lens_v, map_v, schur_v, coup_v, coarse_v, coarse_p,
    fields0, sent0, fields, sent, target, sign_mask, tmp, tmp2,
    meta, tiles_a, tiles_b, coup_a, coup_x, own_w, next_w,
    high_mask, low_hot, gather_hi, gather_lo, acc_v, coarse_b, products,
    round1, round2, round3,
    local_sem, send_sem, recv_sem,
):
    g, d = lax.axis_index("grp"), lax.axis_index("dev")
    lane = iota((8, FD), 1)
    lane1 = iota((1, FD), 1)

    loads = [
        pltpu.make_async_copy(gap_hbm, gap_v, local_sem.at[0]),
        pltpu.make_async_copy(wgt_hbm, wgt_v, local_sem.at[1]),
        pltpu.make_async_copy(links_hbm, links_v, local_sem.at[2]),
        pltpu.make_async_copy(lens_hbm, lens_v, local_sem.at[3]),
        pltpu.make_async_copy(map_hbm, map_v, local_sem.at[4]),
    ]
    loads += [
        pltpu.make_async_copy(coup_hbm.at[s], coup_v.at[pl.ds(KC * s, KC), :], local_sem.at[5 + s])
        for s in range(SUB)
    ]
    loads.append(pltpu.make_async_copy(coarse_hbm, coarse_v, local_sem.at[9]))
    loads += [
        pltpu.make_async_copy(
            schur_hbm.at[s], schur_v.at[pl.ds(768 * s, 768), :], local_sem.at[10 + s]
        )
        for s in range(SUB)
    ]

    barrier = pltpu.get_barrier_semaphore()

    def greet(axis, n):
        def body(k, c):
            t = lax.rem(lax.axis_index(axis) + k, n)
            pl.semaphore_signal(barrier, inc=1, device_id={axis: t}, device_id_type=MESH)
            return c

        lax.fori_loop(1, n, body, 0)

    own_rows = pl.ds(pl.multiple_of(4 * d, 4), 4)
    for buf in [fields0.at[i] for i in range(2)] + [fields.at[i] for i in range(ITERS)]:
        buf[own_rows, :] = jnp.zeros((4, FD), F32)
        buf[160:256, :] = jnp.zeros((96, FD), F32)
    meta[32:128, :] = jnp.zeros((96, FD), F32)
    greet("dev", N_DEV)
    greet("grp", N_GRP)
    for load in loads:
        load.start()

    def send(src, dst, sem, axis, t):
        pltpu.make_async_remote_copy(
            src_ref=src, dst_ref=dst, send_sem=send_sem.at[sem], recv_sem=recv_sem.at[sem],
            device_id={axis: t}, device_id_type=MESH,
        ).start()

    def send_all(axis, n, src_of, dst, sem):
        def body(k, c):
            t = lax.rem(lax.axis_index(axis) + k, n)
            send(src_of(t), dst, sem, axis, t)
            return c

        lax.fori_loop(1, n, body, 0)

    acc_v[...] = jnp.zeros_like(acc_v)
    tmp[...] = jnp.zeros_like(tmp)
    tmp2[...] = jnp.zeros_like(tmp2)

    for load in loads[:5]:
        load.wait()
    links = links_v[...].astype(F32)
    tmp[0:SUB, 0:KC] = map_v[...].astype(F32)
    tmp2[0:SUB, 0:4] = links
    map_rows, link_rows = tmp[...], tmp2[...]
    meta_row = jnp.zeros((1, FD), F32)
    for s in range(SUB):
        meta_row += pltpu.roll(map_rows, KC * s, 1)[s : s + 1] if s else map_rows[0:1]
        meta_row += pltpu.roll(link_rows, CK + 4 * s, 1)[s : s + 1]
    meta[pl.ds(d, 1), :] = meta_row

    plus_dev = jnp.floor(links[0:1, 0:1] * 0.25)
    to_plus = (iota((N_DEV * SUB, FD), 0) // SUB).astype(F32) == plus_dev

    def chosen(values):
        first = jnp.concatenate([values[8:12]] * 32, axis=0)
        second = jnp.concatenate([values[12:16]] * 32, axis=0)
        return jnp.where(to_plus, first, second)

    own0 = []
    for i, src in enumerate((gap_v, wgt_v)):
        for f in range(FACES):
            fields0[i, 128 + 4 * f : 132 + 4 * f, :] = src[:, FD * f : FD * (f + 1)]
        values = fields0[i, 128:152, :]
        own0.append(values)
        sent0[i] = chosen(values)

    up, down = lax.rem(g + 1, N_GRP), lax.rem(g + N_GRP - 1, N_GRP)
    pl.semaphore_wait(barrier, N_DEV + N_GRP - 2)

    def send_fields(buf, out, sem):
        send_all(
            "dev", N_DEV,
            lambda t: out.at[pl.ds(pl.multiple_of(4 * t, 4), 4), :],
            buf.at[pl.ds(pl.multiple_of(4 * d, 4), 4), :], sem,
        )
        send(buf.at[pl.ds(132, 4), :], buf.at[pl.ds(152, 4), :], sem, "grp", down)
        send(buf.at[pl.ds(128, 4), :], buf.at[pl.ds(156, 4), :], sem, "grp", up)

    def await_fields(buf, sems, sem):
        await_bytes(buf.at[pl.ds(0, 4 * (N_DEV + 1)), :], sems.at[sem])

    S_F0, S_META, S_TA, S_TB, S_CX, S_F, S_R1, S_R2, S_R3 = 0, 2, 3, 4, 5, 6, 9, 12, 15

    for i in range(2):
        send_fields(fields0.at[i], sent0.at[i], S_F0 + i)
    own_meta = meta.at[pl.ds(d, 1), :]
    send_all("dev", N_DEV, lambda t: own_meta, own_meta, S_META)
    send(own_meta, meta.at[pl.ds(32, 1), :], S_META, "grp", down)
    send(own_meta, meta.at[pl.ds(33, 1), :], S_META, "grp", up)
    for load in loads[5:9]:
        load.wait()
    for j in range(PIECES):
        @pl.when(d != j)
        def _():
            send(
                coup_v.at[pl.ds(8 * (j % 12), 8), pl.ds(FD * (2 + j // 12), FD)],
                tiles_a.at[pl.ds(pl.multiple_of(8 * d, 8), 8), :], S_TA, "dev", j,
            )
    send(coup_v.at[:, pl.ds(FD, FD)], coup_x.at[0], S_CX, "grp", down)
    send(coup_v.at[:, pl.ds(0, FD)], coup_x.at[1], S_CX, "grp", up)

    row24 = iota((ROWS, FD), 0)
    row_of_lane = jnp.where(
        iota((ROWS, ROWS * FD), 1) // FD == iota((ROWS, ROWS * FD), 0), 1.0, 0.0
    ).astype(BF16)
    sign = (1 - 2 * (lax.rem(row24 // 4, 2))).astype(F32)
    sign_mask[0:8, :] = sign[0:8]
    lens = lens_v[...]
    for k in range(4):
        live = iota((SUB, FD), 1) < lens[:, k : k + 1]
        sign_mask[8 + 4 * k : 12 + 4 * k, :] = jnp.where(live, 1.0 - 2.0 * (k % 2), 0.0)
    jump_sign = sign_mask[...]
    slot = iota((SUB, FD), 0).astype(F32)
    slot_of = links - 4.0 * jnp.floor(links * 0.25)
    ones4 = jnp.ones((SUB, FD), F32)
    target[0:4, :] = slot + 152.0
    target[4:8, :] = slot + 156.0
    target[8:12, :] = ones4 * links[:, 0:1]
    target[12:16, :] = ones4 * links[:, 1:2]
    target[16:20, :] = ones4 * (slot_of[:, 2:3] + 148.0)
    target[20:24, :] = ones4 * (slot_of[:, 3:4] + 144.0)
    targets = jnp.concatenate([target[...]] * 2, axis=1)
    opposite_hot = (targets == iota((ROWS, 256), 1).astype(F32)).astype(BF16)

    loads[9].wait()
    coarse_p[...] = jnp.zeros_like(coarse_p)
    for j in range(HI):
        coarse_p[:, FD * j : FD * j + LO] = coarse_v[:, LO * j : LO * (j + 1)]
    for f in range(FACES):
        for s in range(SUB):
            r = f * SUB + s
            own_w[f, KC * s : KC * (s + 1), :] = (
                coup_v[KC * s : KC * (s + 1), FD * f : FD * (f + 1)] * jump_sign[r : r + 1]
            )

    for i in range(2):
        await_fields(fields0.at[i], recv_sem, S_F0 + i)
    residual = jump_sign * (own0[0] - pick_rows(opposite_hot, fields0[0]))
    scaling = own0[1] + pick_rows(opposite_hot, fields0[1])
    scaled = scaling * residual
    result = jnp.zeros_like(residual)
    direction = image_dir = local_dir = None
    coarse_dir = norm_before = curve_before = None

    for it in range(ITERS):
        load_now = sign * scaled
        for s in range(SUB):
            part = jnp.zeros((KC, FD), F32)
            for f in range(FACES):
                r = f * SUB + s
                part += coup_v[KC * s : KC * (s + 1), FD * f : FD * (f + 1)] * load_now[r : r + 1]
            acc_v[KC * s : KC * (s + 1), :] = part
        r1, r2, r3 = round1.at[it], round2.at[it], round3.at[it]
        r1[pl.ds(d, 1), :] = lane_sums(acc_v[...])
        own = r1.at[pl.ds(d, 1), :]
        send_all("dev", N_DEV, lambda t: own, own, S_R1 + it)

        if it == 0:
            for load in loads[10:]:
                load.wait()
        for s in range(SUB):
            rows_of_load = [load_now[h * SUB + s : h * SUB + s + 1] for h in range(FACES)]

            def block(f, c):
                rows = pl.ds(pl.multiple_of(768 * s + FD * f, FD), FD)
                part = schur_v[rows, 0:FD] * rows_of_load[0]
                for h in range(1, FACES):
                    part += schur_v[rows, FD * h : FD * (h + 1)] * rows_of_load[h]
                products[:, pl.ds(pl.multiple_of(FD * (f * SUB + s), FD), FD)] = part
                return c

            lax.fori_loop(0, FACES, block, 0)
        response = sum(dot_nt(row_of_lane, part) for part in split(products[...], 2))
        buf, out = fields.at[it], sent.at[it]
        buf[128:152, :] = response
        out[...] = chosen(response)
        send_fields(buf, out, S_F + it)
        norm_part = 0.5 * total(residual * scaled)
        curve_part = total(load_now * response)
        cross_part = None
        if it:
            cross_part = total(load_now * local_dir + sign * direction * response)

        if it == 0:
            await_bytes(meta.at[pl.ds(0, N_DEV + 1), :], recv_sem.at[S_META])
            table = meta[...]
            high = jnp.floor((table + 0.5) * (1.0 / LO))
            low = table - LO * high
            hi_rows = iota((HI, FD), 0).astype(F32)
            lo_rows = iota((FD, FD), 0).astype(F32)
            for j in range(N_DEV):
                cols = slice(FD * j, FD * (j + 1))
                high_mask[:, cols] = jnp.where(hi_rows == high[j : j + 1], 1.0, 0.0)
                low_hot[:, cols] = jnp.where(lo_rows == low[j : j + 1], 1.0, 0.0).astype(BF16)

            @pl.when(d < PIECES)
            def _():
                tiles_a[pl.ds(pl.multiple_of(8 * d, 8), 8), :] = coup_v[
                    pl.ds(pl.multiple_of(8 * lax.rem(d, 12), 8), 8),
                    pl.ds(pl.multiple_of(FD * (2 + d // 12), FD), FD),
                ]
                await_bytes(tiles_a.at[pl.ds(0, 8 * (N_DEV - 1)), :], recv_sem.at[S_TA])
                spread = jnp.where(
                    iota((256, FD), 0) // 8 == iota((256, FD), 1), 1.0, 0.0
                ).astype(BF16)
                wanted = dot(spread, table.astype(BF16))
                which = CK + 1 - d // 12
                source = jnp.sum(
                    jnp.where(iota((256, FD), 1) == which, wanted, 0.0), axis=1, keepdims=True
                )
                source = 8.0 * jnp.floor(source * 0.25) + lax.rem(
                    iota((256, 1), 0), 8
                ).astype(F32)
                hot = jnp.where(iota((256, 256), 1).astype(F32) == source, 1.0, 0.0).astype(BF16)
                tiles_b[...] = pick_rows(hot, tiles_a[...])
                here = pl.ds(pl.multiple_of(8 * d, 8), 8)
                coup_a[here, :] = tiles_b[here, :]
                send_all(
                    "dev", N_DEV,
                    lambda t: tiles_b.at[pl.ds(pl.multiple_of(8 * t, 8), 8), :],
                    coup_a.at[here, :], S_TB,
                )

        await_bytes(r1.at[pl.ds(0, N_DEV - 1), :], recv_sem.at[S_R1 + it])
        corner = r1[...]
        top = corner.astype(BF16).astype(F32)
        rest = corner - top
        summed = jnp.zeros((2 * HI, FD), F32)
        for c in range(N_DEV // 2):
            pieces = []
            for source in (top, rest):
                pieces.append(
                    jnp.concatenate(
                        [
                            high_mask[:, FD * j : FD * (j + 1)] * source[j : j + 1]
                            for j in (2 * c, 2 * c + 1)
                        ],
                        axis=1,
                    )
                )
            both = jnp.concatenate(pieces, axis=0).astype(BF16)
            summed += dot_nt(both, low_hot[:, 256 * c : 256 * (c + 1)])
        slab_rhs = summed[0:HI] + summed[HI:]
        coarse_b[...] = slab_rhs
        part = jnp.zeros((CK, FD), F32)
        for j in range(HI):
            part += coarse_p[:, FD * j : FD * (j + 1)] * slab_rhs[j : j + 1]
        acc_v[0:CK, :] = part
        row = lane_sums(acc_v[...])
        row = jnp.where(lane1 == LO, norm_part, row)
        row = jnp.where(lane1 == LO + 1, curve_part, row)
        if it:
            row = jnp.where(lane1 == LO + 2, cross_part, row)
        r2[pl.ds(2 * g, 1), :] = row
        r2[pl.ds(2 * g + 1, 1), :] = coarse_b[pl.ds(d, 1), :]
        mine = r2.at[pl.ds(pl.multiple_of(2 * g, 2), 2), :]
        send_all("grp", N_GRP, lambda t: mine, mine, S_R2 + it)

        if it == 0:
            columns = table.T[0:CK]
            lane_f = iota((CK, FD), 1).astype(F32)

            def column(device):
                return jnp.sum(jnp.where(lane_f == device, columns, 0.0), axis=1, keepdims=True)

            def permuted(values, k):
                groups = []
                for s in range(SUB):
                    got = jnp.zeros((KC, FD), F32)
                    for j in range(SUB):
                        same = slot_of[s : s + 1, k : k + 1] == float(j)
                        got = jnp.where(same, values[KC * j : KC * (j + 1)], got)
                    groups.append(got)
                return jnp.concatenate(groups, axis=0)

            wide = jnp.zeros((CK, FD), F32)
            own_map = column(d.astype(F32)) + wide
            minus_dev = jnp.floor(links[0:1, 1:2] * 0.25)
            maps = [
                own_map,
                column(32.0) + wide,
                column(33.0) + wide,
                permuted(column(plus_dev) + wide, 0),
                permuted(column(minus_dev) + wide, 1),
                permuted(own_map, 2),
                permuted(own_map, 3),
            ]
            for i, m in enumerate(maps):
                high = jnp.floor((m + 0.5) * (1.0 / LO))
                rows = slice(CK * i, CK * (i + 1))
                gather_hi[rows, :] = jnp.where(high == lane_f, 1.0, 0.0).astype(BF16)
                gather_lo[rows, :] = jnp.where(m - LO * high == lane_f, 1.0, 0.0)

        await_bytes(r2.at[pl.ds(0, 2 * (N_GRP - 1)), :], recv_sem.at[S_R2 + it])
        pairs = r2[...]
        even = lax.rem(iota((2 * N_GRP, FD), 0), 2) == 0
        sol_row = jnp.sum(jnp.where(even, pairs, 0.0), axis=0, keepdims=True)
        rhs_row = jnp.sum(jnp.where(even, 0.0, pairs), axis=0, keepdims=True)
        row = jnp.where(
            lane1 == LO + 3, jnp.sum(sol_row * rhs_row, axis=1, keepdims=True), sol_row
        )
        if it:
            row = jnp.where(
                lane1 == LO + 4, jnp.sum(sol_row * coarse_dir, axis=1, keepdims=True), row
            )
        r3[pl.ds(d, 1), :] = row
        own3 = r3.at[pl.ds(d, 1), :]
        send_all("dev", N_DEV, lambda t: own3, own3, S_R3 + it)

        await_fields(buf, recv_sem, S_F + it)
        local_jump = jump_sign * (response - pick_rows(opposite_hot, buf[...]))
        if it == 0:
            @pl.when(d < PIECES)
            def _():
                await_bytes(coup_a.at[pl.ds(0, 8 * (PIECES - 1)), :], recv_sem.at[S_TB])

            @pl.when(d >= PIECES)
            def _():
                await_bytes(coup_a.at[pl.ds(0, 8 * PIECES), :], recv_sem.at[S_TB])

            await_bytes(coup_x, recv_sem.at[S_CX])
            beyond = [
                coup_x[0],
                coup_x[1],
                permuted(coup_a[CK : 2 * CK, :], 0),
                permuted(coup_a[0:CK, :], 1),
                permuted(coup_v[:, FD * 5 : FD * 6], 2),
                permuted(coup_v[:, FD * 4 : FD * 5], 3),
            ]
            for f in range(FACES):
                for s in range(SUB):
                    r = f * SUB + s
                    next_w[f, KC * s : KC * (s + 1), :] = (
                        -jump_sign[r : r + 1] * beyond[f][KC * s : KC * (s + 1)]
                    )

        await_bytes(r3.at[pl.ds(0, N_DEV - 1), :], recv_sem.at[S_R3 + it])
        coarse_sol = r3[...]
        sums = jnp.sum(coarse_sol, axis=0, keepdims=True)
        norm_now = sums[:, LO : LO + 1]
        curve = sums[:, LO + 1 : LO + 2] + sums[:, LO + 3 : LO + 4]
        padded = jnp.concatenate([coarse_sol, jnp.zeros((FD - HI, FD), F32)], axis=0)
        at_corner = []
        sol_parts = split(padded, 3)
        for i in range(7):
            rows = slice(CK * i, CK * (i + 1))
            hot = gather_hi[rows, :]
            got = sum(dot(hot, p) for p in sol_parts) * gather_lo[rows, :]
            at_corner.append(jnp.sum(got, axis=1, keepdims=True))
        for f in range(FACES):
            both = own_w[f] * at_corner[0] + next_w[f] * at_corner[1 + f]
            for s in range(SUB):
                r = f * SUB + s
                target[r : r + 1, :] = jnp.sum(
                    both[KC * s : KC * (s + 1)], axis=0, keepdims=True
                )
        image = local_jump + target[...]

        if it == 0:
            direction, image_dir, local_dir, coarse_dir = scaled, image, response, rhs_row
        else:
            ratio = norm_now / norm_before
            cross = sums[:, LO + 2 : LO + 3] + 2.0 * sums[:, LO + 4 : LO + 5]
            curve = curve + ratio * cross + ratio * ratio * curve_before
            direction = scaled + ratio * direction
            image_dir = image + ratio * image_dir
            local_dir = response + ratio * local_dir
            coarse_dir = rhs_row + ratio * coarse_dir
        step = norm_now / curve
        norm_before, curve_before = norm_now, curve
        result = result + step * direction
        residual = residual - step * image_dir
        scaled = scaling * residual

    for f in range(FACES):
        x_out[:, FD * f : FD * (f + 1)] = result[4 * f : 4 * f + 4]
        r_out[:, FD * f : FD * (f + 1)] = residual[4 * f : 4 * f + 4]

    for i in range(2):
        await_fields(fields0.at[i], send_sem, S_F0 + i)
    await_bytes(meta.at[pl.ds(0, N_DEV + 1), :], send_sem.at[S_META])

    @pl.when(d < PIECES)
    def _():
        await_bytes(tiles_a.at[pl.ds(0, 8 * (PIECES - 1)), :], send_sem.at[S_TA])
        await_bytes(tiles_b.at[pl.ds(0, 8 * (N_DEV - 1)), :], send_sem.at[S_TB])

    @pl.when(d >= PIECES)
    def _():
        await_bytes(tiles_a.at[pl.ds(0, 8 * PIECES), :], send_sem.at[S_TA])

    await_bytes(coup_x, send_sem.at[S_CX])
    for it in range(ITERS):
        await_fields(fields.at[it], send_sem, S_F + it)
        await_bytes(round1.at[it].at[pl.ds(0, N_DEV - 1), :], send_sem.at[S_R1 + it])
        await_bytes(round2.at[it].at[pl.ds(0, 2 * (N_GRP - 1)), :], send_sem.at[S_R2 + it])
        await_bytes(round3.at[it].at[pl.ds(0, N_DEV - 1), :], send_sem.at[S_R3 + it])


def per_device(*args):
    vmem = lambda *shape: pltpu.VMEM(shape, F32)
    field = jax.ShapeDtypeStruct((SUB, FACES * FD), F32)
    return pl.pallas_call(
        kernel,
        out_shape=(field, field),
        in_specs=[pl.BlockSpec(memory_space=pltpu.HBM)] * 8,
        out_specs=(pl.BlockSpec(memory_space=pltpu.VMEM),) * 2,
        scratch_shapes=[
            vmem(SUB, 768), vmem(SUB, 768),
            pltpu.VMEM((SUB, 4), jnp.int32), pltpu.VMEM((SUB, 4), jnp.int32),
            pltpu.VMEM((SUB, KC), jnp.int32),
            vmem(SUB * 768, 768), vmem(CK, 768), vmem(CK, 3072), vmem(CK, HI * FD),
            vmem(2, 256, FD), vmem(2, 128, FD),
            vmem(ITERS, 256, FD), vmem(ITERS, 128, FD),
            vmem(ROWS, FD), vmem(ROWS, FD), vmem(8, FD), vmem(8, FD),
            vmem(FD, FD), vmem(256, FD), vmem(256, FD), vmem(2 * CK, FD), vmem(2, CK, FD),
            vmem(FACES, CK, FD), vmem(FACES, CK, FD),
            vmem(HI, HI * FD), pltpu.VMEM((FD, HI * FD), BF16),
            pltpu.VMEM((7 * CK, FD), BF16), vmem(7 * CK, FD), vmem(FD, FD), vmem(HI, FD), vmem(FD, ROWS * FD),
            vmem(ITERS, N_DEV, FD), vmem(ITERS, 2 * N_GRP, FD), vmem(ITERS, N_DEV, FD),
            pltpu.SemaphoreType.DMA((14,)),
            pltpu.SemaphoreType.DMA((18,)),
            pltpu.SemaphoreType.DMA((18,)),
        ],
        compiler_params=pltpu.CompilerParams(
            collective_id=0, has_side_effects=True, vmem_limit_bytes=63 * 1024 * 1024
        ),
    )(*args)


def solution(mesh):
    return jax.shard_map(
        per_device,
        mesh=mesh,
        in_specs=(
            P(("grp", "dev"), None),
            P(("grp", "dev"), None),
            P("dev", None),
            P("dev", None),
            P(("grp", "dev"), None, None),
            P(("grp", "dev"), None),
            P(("grp", "dev"), None, None),
            P("dev", None),
        ),
        out_specs=(P(("grp", "dev"), None), P(("grp", "dev"), None)),
        check_vma=False,
    )
```

```python
import functools

import jax
import jax.numpy as jnp
from jax import lax
from jax.experimental import pallas as pl
from jax.experimental.pallas import tpu as pltpu
from jax.sharding import PartitionSpec as P

ITERS = 3
MESH = pl.DeviceIdType.MESH
F32 = jnp.float32
BF16 = jnp.bfloat16
N_GRP, N_DEV = 8, 32
SUB, KC, FD, FACES = 4, 24, 128, 6
ROWS = SUB * FACES
CK = SUB * KC
HI, LO = 32, 96
FAR = 8
PIECES = 2 * CK // 8


def iota(shape, dim):
    return lax.broadcasted_iota(jnp.int32, shape, dim)


def split(x, parts):
    out = []
    for _ in range(parts - 1):
        top = x.astype(BF16)
        out.append(top)
        x = x - top.astype(F32)
    out.append(x.astype(BF16))
    return out


def dot(a, b):
    return jnp.dot(a, b, preferred_element_type=F32)


def dot_nt(a, b):
    return lax.dot_general(a, b, (((1,), (1,)), ((), ())), preferred_element_type=F32)


def pick_rows(one_hot, x):
    return sum(dot(one_hot, part) for part in split(x, 2))


def lane_sums(x):
    ones = jnp.ones((8, x.shape[1]), BF16)
    return sum(dot_nt(ones, part) for part in split(x, 2))[0:1]


def total(x):
    return jnp.sum(jnp.sum(x, axis=0, keepdims=True), axis=1, keepdims=True)


def await_bytes(ref, sem):
    pltpu.make_async_copy(ref, ref, sem).wait()


def far_first(i, n):
    return n // 2 + (1 - 2 * lax.rem(i, 2)) * ((i + 1) // 2)


def kernel(
    gap_hbm, wgt_hbm, links_hbm, lens_hbm, schur_hbm, map_hbm, coup_hbm, coarse_hbm,
    out_ref,
    gap_v, wgt_v, links_v, lens_v, map_v, schur_v, coup_v, coarse_v, coarse_p,
    fields0, sent0, fields, sent, target, sign_mask, tmp, tmp2,
    meta, slots, tiles_a, tiles_b, coup_a, coup_x, own_w, next_w,
    high_mask, low_hot, gather_hi, gather_lo, acc_v, coarse_b, products, placed,
    round1, round2, round3,
    local_sem, send_sem, recv_sem,
):
    g, d = lax.axis_index("grp"), lax.axis_index("dev")
    lane = iota((8, FD), 1)
    lane1 = iota((1, FD), 1)

    loads = [
        pltpu.make_async_copy(gap_hbm, gap_v, local_sem.at[0]),
        pltpu.make_async_copy(wgt_hbm, wgt_v, local_sem.at[1]),
        pltpu.make_async_copy(links_hbm, links_v, local_sem.at[2]),
        pltpu.make_async_copy(lens_hbm, lens_v, local_sem.at[3]),
        pltpu.make_async_copy(map_hbm, map_v, local_sem.at[4]),
    ]
    loads += [
        pltpu.make_async_copy(coup_hbm.at[s], coup_v.at[pl.ds(KC * s, KC), :], local_sem.at[5 + s])
        for s in range(SUB)
    ]
    loads.append(pltpu.make_async_copy(coarse_hbm, coarse_v, local_sem.at[9]))
    loads += [
        pltpu.make_async_copy(
            schur_hbm.at[s], schur_v.at[pl.ds(768 * s, 768), :], local_sem.at[10 + s]
        )
        for s in range(SUB)
    ]

    barrier = pltpu.get_barrier_semaphore()

    def offsets(i):
        return far_first(i // 4, 8), far_first(lax.rem(i, 4), 4)

    def slab_target(i):
        dz, dy = offsets(i)
        return lax.rem(d // 4 + dz, 8) * 4 + lax.rem(lax.rem(d, 4) + dy, 4)

    def slab_source(i):
        dz, dy = offsets(i)
        return lax.rem(d // 4 + 8 - dz, 8) * 4 + lax.rem(lax.rem(d, 4) + 4 - dy, 4)

    def each(axis, first, last, act):
        def body(i, c):
            if axis == "dev":
                act(slab_target(i), i)
            else:
                act(lax.rem(g + far_first(i, N_GRP), N_GRP), i)
            return c

        lax.fori_loop(first, last, body, 0)

    def greet(axis, n):
        def act(t, i):
            pl.semaphore_signal(barrier, inc=1, device_id={axis: t}, device_id_type=MESH)

        each(axis, 0, n - 1, act)

    own_rows = pl.ds(pl.multiple_of(4 * d, 4), 4)
    for buf in [fields0.at[i] for i in range(2)] + [fields.at[i] for i in range(ITERS)]:
        buf[own_rows, :] = jnp.zeros((4, FD), F32)
    meta[32:128, :] = jnp.zeros((96, FD), F32)
    slots[32:128, :] = jnp.zeros((96, FD), F32)
    greet("dev", N_DEV)
    greet("grp", N_GRP)
    for load in loads:
        load.start()

    def send(src, dst, sem, axis, t):
        pltpu.make_async_remote_copy(
            src_ref=src, dst_ref=dst, send_sem=send_sem.at[sem], recv_sem=recv_sem.at[sem],
            device_id={axis: t}, device_id_type=MESH,
        ).start()

    def send_all(axis, n, src_of, dst, sem):
        each(axis, 0, n - 1, lambda t, i: send(src_of(t), dst, sem, axis, t))

    acc_v[...] = jnp.zeros_like(acc_v)
    tmp[...] = jnp.zeros_like(tmp)
    tmp2[...] = jnp.zeros_like(tmp2)

    for load in loads[:5]:
        load.wait()
    links = links_v[...].astype(F32)
    tmp[0:SUB, 0:KC] = map_v[...].astype(F32)
    tmp2[0:SUB, 0:4] = links
    map_rows, link_rows = tmp[...], tmp2[...]
    meta_row = jnp.zeros((1, FD), F32)
    for s in range(SUB):
        meta_row += pltpu.roll(map_rows, KC * s, 1)[s : s + 1] if s else map_rows[0:1]
        meta_row += pltpu.roll(link_rows, CK + 4 * s, 1)[s : s + 1]
    meta[pl.ds(d, 1), :] = meta_row

    plus_dev = jnp.floor(links[0:1, 0:1] * 0.25)
    to_plus = (iota((N_DEV * SUB, FD), 0) // SUB).astype(F32) == plus_dev

    def chosen(values):
        first = jnp.concatenate([values[8:12]] * 32, axis=0)
        second = jnp.concatenate([values[12:16]] * 32, axis=0)
        return jnp.where(to_plus, first, second)

    own0 = []
    for i, src in enumerate((gap_v, wgt_v)):
        for f in range(FACES):
            fields0[i, 128 + 4 * f : 132 + 4 * f, :] = src[:, FD * f : FD * (f + 1)]
        values = fields0[i, 128:152, :]
        own0.append(values)
        sent0[i] = chosen(values)

    up, down = lax.rem(g + 1, N_GRP), lax.rem(g + N_GRP - 1, N_GRP)
    pl.semaphore_wait(barrier, N_DEV + N_GRP - 2)

    def send_fields(buf, out, sem):
        send_all(
            "dev", N_DEV,
            lambda t: out.at[pl.ds(pl.multiple_of(4 * t, 4), 4), :],
            buf.at[pl.ds(pl.multiple_of(4 * d, 4), 4), :], sem,
        )
        send(buf.at[pl.ds(132, 4), :], buf.at[pl.ds(152, 4), :], sem, "grp", down)
        send(buf.at[pl.ds(128, 4), :], buf.at[pl.ds(156, 4), :], sem, "grp", up)

    def await_fields(buf, sems, sem):
        await_bytes(buf.at[pl.ds(0, 4 * (N_DEV + 1)), :], sems.at[sem])

    S_F0, S_META, S_TA, S_TB, S_CX, S_F, S_R1, S_R2, S_R3, S_NEAR = (
        0, 2, 3, 4, 5, 6, 9, 12, 15, 18
    )

    for i in range(2):
        send_fields(fields0.at[i], sent0.at[i], S_F0 + i)
    own_meta = meta.at[pl.ds(d, 1), :]
    send_all("dev", N_DEV, lambda t: own_meta, own_meta, S_META)
    send(own_meta, meta.at[pl.ds(32, 1), :], S_META, "grp", down)
    send(own_meta, meta.at[pl.ds(33, 1), :], S_META, "grp", up)
    for load in loads[5:9]:
        load.wait()
    for j in range(PIECES):
        @pl.when(d != j)
        def _():
            send(
                coup_v.at[pl.ds(8 * (j % 12), 8), pl.ds(FD * (2 + j // 12), FD)],
                tiles_a.at[pl.ds(pl.multiple_of(8 * d, 8), 8), :], S_TA, "dev", j,
            )
    send(coup_v.at[:, pl.ds(FD, FD)], coup_x.at[0], S_CX, "grp", down)
    send(coup_v.at[:, pl.ds(0, FD)], coup_x.at[1], S_CX, "grp", up)

    row24 = iota((ROWS, FD), 0)
    row_of_lane = jnp.where(
        iota((ROWS, ROWS * FD), 1) // FD == iota((ROWS, ROWS * FD), 0), 1.0, 0.0
    ).astype(BF16)
    sign = (1 - 2 * (lax.rem(row24 // 4, 2))).astype(F32)
    sign_mask[0:8, :] = sign[0:8]
    lens = lens_v[...]
    for k in range(4):
        live = iota((SUB, FD), 1) < lens[:, k : k + 1]
        sign_mask[8 + 4 * k : 12 + 4 * k, :] = jnp.where(live, 1.0 - 2.0 * (k % 2), 0.0)
    jump_sign = sign_mask[...]
    slot = iota((SUB, FD), 0).astype(F32)
    slot_of = links - 4.0 * jnp.floor(links * 0.25)
    ones4 = jnp.ones((SUB, FD), F32)
    target[0:4, :] = slot + 152.0
    target[4:8, :] = slot + 156.0
    target[8:12, :] = ones4 * links[:, 0:1]
    target[12:16, :] = ones4 * links[:, 1:2]
    target[16:20, :] = ones4 * (slot_of[:, 2:3] + 148.0)
    target[20:24, :] = ones4 * (slot_of[:, 3:4] + 144.0)
    targets = target[...][:, 0:1]
    opposite_hot = jnp.where(targets == iota((ROWS, 160), 1).astype(F32), 1.0, 0.0).astype(BF16)

    loads[9].wait()
    coarse_p[...] = jnp.zeros_like(coarse_p)
    for j in range(HI):
        coarse_p[:, FD * j : FD * j + LO] = coarse_v[:, LO * j : LO * (j + 1)]
    for f in range(FACES):
        for s in range(SUB):
            r = f * SUB + s
            own_w[f, KC * s : KC * (s + 1), :] = (
                coup_v[KC * s : KC * (s + 1), FD * f : FD * (f + 1)] * jump_sign[r : r + 1]
            )

    for i in range(2):
        await_fields(fields0.at[i], recv_sem, S_F0 + i)
    residual = jump_sign * (own0[0] - pick_rows(opposite_hot, fields0[0]))
    scaling = own0[1] + pick_rows(opposite_hot, fields0[1])
    scaled = scaling * residual
    result = jnp.zeros_like(residual)
    direction = image_dir = local_dir = None
    coarse_dir = norm_before = curve_before = None

    def scattered(loads_of, first, last):
        parts = [part.astype(F32) for part in split(loads_of[first:last, :], 2)]
        for j in range(first, last):
            for q in range(2):
                placed[HI * q : HI * (q + 1), FD * j : FD * (j + 1)] = (
                    high_mask[:, FD * j : FD * (j + 1)] * parts[q][j - first : j - first + 1]
                ).astype(BF16)
        return dot(placed[:, FD * first : FD * last], low_hot[FD * first : FD * last, :])

    def sends_done(it):
        if it < 0:
            for i in range(2):
                await_fields(fields0.at[i], send_sem, S_F0 + i)
            await_bytes(meta.at[pl.ds(0, N_DEV + 1), :], send_sem.at[S_META])

            @pl.when(d < PIECES)
            def _():
                await_bytes(tiles_a.at[pl.ds(0, 8 * (PIECES - 1)), :], send_sem.at[S_TA])

            @pl.when(d >= PIECES)
            def _():
                await_bytes(tiles_a.at[pl.ds(0, 8 * PIECES), :], send_sem.at[S_TA])

            await_bytes(coup_x, send_sem.at[S_CX])
            return
        if it == 0:
            @pl.when(d < PIECES)
            def _():
                await_bytes(tiles_b.at[pl.ds(0, 8 * (N_DEV - 1)), :], send_sem.at[S_TB])

        await_fields(fields.at[it], send_sem, S_F + it)
        one = round1.at[it]
        await_bytes(one.at[pl.ds(0, FAR), :], send_sem.at[S_R1 + it])
        await_bytes(one.at[pl.ds(0, N_DEV - 1 - FAR), :], send_sem.at[S_NEAR + it])
        await_bytes(round2.at[it].at[pl.ds(0, 2 * (N_GRP - 1)), :], send_sem.at[S_R2 + it])
        await_bytes(round3.at[it].at[pl.ds(0, N_DEV - 1), :], send_sem.at[S_R3 + it])

    for it in range(ITERS):
        load_now = sign * scaled
        for s in range(SUB):
            part = jnp.zeros((KC, FD), F32)
            for f in range(FACES):
                r = f * SUB + s
                part += coup_v[KC * s : KC * (s + 1), FD * f : FD * (f + 1)] * load_now[r : r + 1]
            acc_v[KC * s : KC * (s + 1), :] = part
        r1, r2, r3 = round1.at[it], round2.at[it], round3.at[it]
        r1[N_DEV - 1 :, :] = lane_sums(acc_v[...])
        own = r1.at[pl.ds(N_DEV - 1, 1), :]
        each("dev", 0, FAR, lambda t, i: send(own, r1.at[pl.ds(i, 1), :], S_R1 + it, "dev", t))
        each(
            "dev", FAR, N_DEV - 1,
            lambda t, i: send(own, r1.at[pl.ds(i, 1), :], S_NEAR + it, "dev", t),
        )

        if it == 0:
            for load in loads[10:]:
                load.wait()
        for s in range(SUB):
            rows_of_load = [load_now[h * SUB + s : h * SUB + s + 1] for h in range(FACES)]

            def block(f, c):
                rows = pl.ds(pl.multiple_of(768 * s + FD * f, FD), FD)
                part = schur_v[rows, 0:FD] * rows_of_load[0]
                for h in range(1, FACES):
                    part += schur_v[rows, FD * h : FD * (h + 1)] * rows_of_load[h]
                products[:, pl.ds(pl.multiple_of(FD * (f * SUB + s), FD), FD)] = part
                return c

            lax.fori_loop(0, FACES, block, 0)
        response = sum(dot_nt(row_of_lane, part) for part in split(products[...], 2))
        buf, out = fields.at[it], sent.at[it]
        buf[128:152, :] = response
        out[...] = chosen(response)
        send_fields(buf, out, S_F + it)
        norm_part = 0.5 * total(residual * scaled)
        curve_part = total(load_now * response)
        cross_part = None
        if it:
            cross_part = total(load_now * local_dir + sign * direction * response)

        if it == 0:
            await_bytes(meta.at[pl.ds(0, N_DEV + 1), :], recv_sem.at[S_META])
            table = meta[...]

            def reorder(i, c):
                slots[pl.ds(i, 1), :] = meta[pl.ds(slab_source(i), 1), :]
                return c

            lax.fori_loop(0, N_DEV, reorder, 0)
            ordered = slots[...]
            high = jnp.floor((ordered + 0.5) * (1.0 / LO))
            low = (ordered - LO * high).T
            hi_rows = iota((HI, FD), 0).astype(F32)
            lo_lanes = iota((FD, FD), 1).astype(F32)
            for j in range(N_DEV):
                cols = slice(FD * j, FD * (j + 1))
                high_mask[:, cols] = jnp.where(hi_rows == high[j : j + 1], 1.0, 0.0)
                low_hot[cols, :] = jnp.where(lo_lanes == low[:, j : j + 1], 1.0, 0.0).astype(BF16)

            @pl.when(d < PIECES)
            def _():
                tiles_a[pl.ds(pl.multiple_of(8 * d, 8), 8), :] = coup_v[
                    pl.ds(pl.multiple_of(8 * lax.rem(d, 12), 8), 8),
                    pl.ds(pl.multiple_of(FD * (2 + d // 12), FD), FD),
                ]
                await_bytes(tiles_a.at[pl.ds(0, 8 * (N_DEV - 1)), :], recv_sem.at[S_TA])
                spread = jnp.where(
                    iota((256, FD), 0) // 8 == iota((256, FD), 1), 1.0, 0.0
                ).astype(BF16)
                wanted = dot(spread, table.astype(BF16))
                which = CK + 1 - d // 12
                source = jnp.sum(
                    jnp.where(iota((256, FD), 1) == which, wanted, 0.0), axis=1, keepdims=True
                )
                source = 8.0 * jnp.floor(source * 0.25) + lax.rem(
                    iota((256, 1), 0), 8
                ).astype(F32)
                hot = jnp.where(iota((256, 256), 1).astype(F32) == source, 1.0, 0.0).astype(BF16)
                tiles_b[...] = pick_rows(hot, tiles_a[...])
                here = pl.ds(pl.multiple_of(8 * d, 8), 8)
                coup_a[here, :] = tiles_b[here, :]
                send_all(
                    "dev", N_DEV,
                    lambda t: tiles_b.at[pl.ds(pl.multiple_of(8 * t, 8), 8), :],
                    coup_a.at[here, :], S_TB,
                )

        sends_done(it - 1)

        await_bytes(r1.at[pl.ds(FAR, N_DEV - 1 - FAR), :], recv_sem.at[S_NEAR + it])
        summed = scattered(r1, FAR, N_DEV)
        await_bytes(r1.at[pl.ds(0, FAR), :], recv_sem.at[S_R1 + it])
        summed += scattered(r1, 0, FAR)
        slab_rhs = summed[0:HI] + summed[HI:]
        coarse_b[...] = slab_rhs
        part = jnp.zeros((CK, FD), F32)
        for j in range(HI):
            part += coarse_p[:, FD * j : FD * (j + 1)] * slab_rhs[j : j + 1]
        acc_v[0:CK, :] = part
        row = lane_sums(acc_v[...])
        row = jnp.where(lane1 == LO, norm_part, row)
        row = jnp.where(lane1 == LO + 1, curve_part, row)
        if it:
            row = jnp.where(lane1 == LO + 2, cross_part, row)
        r2[pl.ds(2 * g, 1), :] = row
        r2[pl.ds(2 * g + 1, 1), :] = coarse_b[pl.ds(d, 1), :]
        mine = r2.at[pl.ds(pl.multiple_of(2 * g, 2), 2), :]
        send_all("grp", N_GRP, lambda t: mine, mine, S_R2 + it)

        if it == 0:
            columns = table.T[0:CK]
            lane_f = iota((CK, FD), 1).astype(F32)

            def column(device):
                return jnp.sum(jnp.where(lane_f == device, columns, 0.0), axis=1, keepdims=True)

            def permuted(values, k):
                groups = []
                for s in range(SUB):
                    got = jnp.zeros((KC, FD), F32)
                    for j in range(SUB):
                        same = slot_of[s : s + 1, k : k + 1] == float(j)
                        got = jnp.where(same, values[KC * j : KC * (j + 1)], got)
                    groups.append(got)
                return jnp.concatenate(groups, axis=0)

            wide = jnp.zeros((CK, FD), F32)
            own_map = column(d.astype(F32)) + wide
            minus_dev = jnp.floor(links[0:1, 1:2] * 0.25)
            maps = [
                own_map,
                column(32.0) + wide,
                column(33.0) + wide,
                permuted(column(plus_dev) + wide, 0),
                permuted(column(minus_dev) + wide, 1),
                permuted(own_map, 2),
                permuted(own_map, 3),
            ]
            for i, m in enumerate(maps):
                high = jnp.floor((m + 0.5) * (1.0 / LO))
                rows = slice(CK * i, CK * (i + 1))
                gather_hi[rows, :] = jnp.where(high == lane_f, 1.0, 0.0).astype(BF16)
                gather_lo[rows, :] = jnp.where(m - LO * high == lane_f, 1.0, 0.0)

        await_bytes(r2.at[pl.ds(0, 2 * (N_GRP - 1)), :], recv_sem.at[S_R2 + it])
        pairs = r2[...]
        even = lax.rem(iota((2 * N_GRP, FD), 0), 2) == 0
        sol_row = jnp.sum(jnp.where(even, pairs, 0.0), axis=0, keepdims=True)
        rhs_row = jnp.sum(jnp.where(even, 0.0, pairs), axis=0, keepdims=True)
        row = jnp.where(
            lane1 == LO + 3, jnp.sum(sol_row * rhs_row, axis=1, keepdims=True), sol_row
        )
        if it:
            row = jnp.where(
                lane1 == LO + 4, jnp.sum(sol_row * coarse_dir, axis=1, keepdims=True), row
            )
        r3[pl.ds(d, 1), :] = row
        own3 = r3.at[pl.ds(d, 1), :]
        send_all("dev", N_DEV, lambda t: own3, own3, S_R3 + it)

        await_fields(buf, recv_sem, S_F + it)
        local_jump = jump_sign * (response - pick_rows(opposite_hot, buf[...]))
        if it == 0:
            @pl.when(d < PIECES)
            def _():
                await_bytes(coup_a.at[pl.ds(0, 8 * (PIECES - 1)), :], recv_sem.at[S_TB])

            @pl.when(d >= PIECES)
            def _():
                await_bytes(coup_a.at[pl.ds(0, 8 * PIECES), :], recv_sem.at[S_TB])

            await_bytes(coup_x, recv_sem.at[S_CX])
            beyond = [
                coup_x[0],
                coup_x[1],
                permuted(coup_a[CK : 2 * CK, :], 0),
                permuted(coup_a[0:CK, :], 1),
                permuted(coup_v[:, FD * 5 : FD * 6], 2),
                permuted(coup_v[:, FD * 4 : FD * 5], 3),
            ]
            for f in range(FACES):
                for s in range(SUB):
                    r = f * SUB + s
                    next_w[f, KC * s : KC * (s + 1), :] = (
                        -jump_sign[r : r + 1] * beyond[f][KC * s : KC * (s + 1)]
                    )

        await_bytes(r3.at[pl.ds(0, N_DEV - 1), :], recv_sem.at[S_R3 + it])
        coarse_sol = r3[...]
        sums = jnp.sum(coarse_sol, axis=0, keepdims=True)
        norm_now = sums[:, LO : LO + 1]
        curve = sums[:, LO + 1 : LO + 2] + sums[:, LO + 3 : LO + 4]
        padded = jnp.concatenate([coarse_sol, jnp.zeros((FD - HI, FD), F32)], axis=0)
        at_corner = []
        sol_parts = split(padded, 2)
        for i in range(7):
            rows = slice(CK * i, CK * (i + 1))
            hot = gather_hi[rows, :]
            got = sum(dot(hot, p) for p in sol_parts) * gather_lo[rows, :]
            at_corner.append(jnp.sum(got, axis=1, keepdims=True))
        for f in range(FACES):
            both = own_w[f] * at_corner[0] + next_w[f] * at_corner[1 + f]
            for s in range(SUB):
                r = f * SUB + s
                target[r : r + 1, :] = jnp.sum(
                    both[KC * s : KC * (s + 1)], axis=0, keepdims=True
                )
        image = local_jump + target[...]

        if it == 0:
            direction, image_dir, local_dir, coarse_dir = scaled, image, response, rhs_row
        else:
            ratio = norm_now / norm_before
            cross = sums[:, LO + 2 : LO + 3] + 2.0 * sums[:, LO + 4 : LO + 5]
            curve = curve + ratio * cross + ratio * ratio * curve_before
            direction = scaled + ratio * direction
            image_dir = image + ratio * image_dir
            local_dir = response + ratio * local_dir
            coarse_dir = rhs_row + ratio * coarse_dir
        step = norm_now / curve
        norm_before, curve_before = norm_now, curve
        result = result + step * direction
        residual = residual - step * image_dir
        scaled = scaling * residual

    for f in range(FACES):
        out_ref[0, :, FD * f : FD * (f + 1)] = result[4 * f : 4 * f + 4]
        out_ref[1, :, FD * f : FD * (f + 1)] = residual[4 * f : 4 * f + 4]

    sends_done(ITERS - 1)


def per_device(*args):
    vmem = lambda *shape: pltpu.VMEM(shape, F32)
    field = jax.ShapeDtypeStruct((2, SUB, FACES * FD), F32)
    both = pl.pallas_call(
        kernel,
        out_shape=field,
        in_specs=[pl.BlockSpec(memory_space=pltpu.HBM)] * 8,
        out_specs=pl.BlockSpec(memory_space=pltpu.VMEM),
        scratch_shapes=[
            vmem(SUB, 768), vmem(SUB, 768),
            pltpu.VMEM((SUB, 4), jnp.int32), pltpu.VMEM((SUB, 4), jnp.int32),
            pltpu.VMEM((SUB, KC), jnp.int32),
            vmem(SUB * 768, 768), vmem(CK, 768), vmem(CK, 3072), vmem(CK, HI * FD),
            vmem(2, 160, FD), vmem(2, 128, FD),
            vmem(ITERS, 160, FD), vmem(ITERS, 128, FD),
            vmem(ROWS, FD), vmem(ROWS, FD), vmem(8, FD), vmem(8, FD),
            vmem(FD, FD), vmem(FD, FD), vmem(256, FD), vmem(256, FD), vmem(2 * CK, FD), vmem(2, CK, FD),
            vmem(FACES, CK, FD), vmem(FACES, CK, FD),
            vmem(HI, HI * FD), pltpu.VMEM((HI * FD, FD), BF16),
            pltpu.VMEM((7 * CK, FD), BF16), vmem(7 * CK, FD), vmem(FD, FD), vmem(HI, FD), vmem(FD, ROWS * FD), pltpu.VMEM((2 * HI, HI * FD), BF16),
            vmem(ITERS, N_DEV, FD), vmem(ITERS, 2 * N_GRP, FD), vmem(ITERS, N_DEV, FD),
            pltpu.SemaphoreType.DMA((14,)),
            pltpu.SemaphoreType.DMA((21,)),
            pltpu.SemaphoreType.DMA((21,)),
        ],
        compiler_params=pltpu.CompilerParams(
            collective_id=0, has_side_effects=True, vmem_limit_bytes=63 * 1024 * 1024
        ),
    )(*args)
    return both[0], both[1]


def solution(mesh):
    return jax.shard_map(
        per_device,
        mesh=mesh,
        in_specs=(
            P(("grp", "dev"), None),
            P(("grp", "dev"), None),
            P("dev", None),
            P("dev", None),
            P(("grp", "dev"), None, None),
            P(("grp", "dev"), None),
            P(("grp", "dev"), None, None),
            P("dev", None),
        ),
        out_specs=(P(("grp", "dev"), None), P(("grp", "dev"), None)),
        check_vma=False,
    )
```

```python
import functools

import jax
import jax.numpy as jnp
from jax import lax
from jax.experimental import pallas as pl
from jax.experimental.pallas import tpu as pltpu
from jax.sharding import PartitionSpec as P

ITERS = 3
MESH = pl.DeviceIdType.MESH
F32 = jnp.float32
BF16 = jnp.bfloat16
N_GRP, N_DEV = 8, 32
SUB, KC, FD, FACES = 4, 24, 128, 6
ROWS = SUB * FACES
CK = SUB * KC
HI, LO = 32, 96
FAR = 8
PIECES = 2 * CK // 8


def iota(shape, dim):
    return lax.broadcasted_iota(jnp.int32, shape, dim)


def split(x, parts):
    out = []
    for _ in range(parts - 1):
        top = x.astype(BF16)
        out.append(top)
        x = x - top.astype(F32)
    out.append(x.astype(BF16))
    return out


def dot(a, b):
    return jnp.dot(a, b, preferred_element_type=F32)


def dot_nt(a, b):
    return lax.dot_general(a, b, (((1,), (1,)), ((), ())), preferred_element_type=F32)


def pick_rows(one_hot, x):
    return sum(dot(one_hot, part) for part in split(x, 2))


def lane_sums(x):
    ones = jnp.ones((8, x.shape[1]), BF16)
    return sum(dot_nt(ones, part) for part in split(x, 2))[0:1]


def total(x):
    return jnp.sum(jnp.sum(x, axis=0, keepdims=True), axis=1, keepdims=True)


def await_bytes(ref, sem):
    pltpu.make_async_copy(ref, ref, sem).wait()


def far_first(i, n):
    return n // 2 + (1 - 2 * lax.rem(i, 2)) * ((i + 1) // 2)


def kernel(
    gap_hbm, wgt_hbm, links_hbm, lens_hbm, schur_hbm, map_hbm, coup_hbm, coarse_hbm,
    out_ref,
    gap_v, wgt_v, links_v, lens_v, map_v, schur_v, coup_v, coarse_v, coarse_p,
    fields0, sent0, fields, sent, target, sign_mask, tmp, tmp2,
    meta, slots, tiles_a, tiles_b, coup_a, coup_x, own_w, next_w,
    high_mask, low_hot, gather_hi, gather_lo, acc_v, products, placed,
    round1, round2, round3,
    local_sem, send_sem, recv_sem,
):
    g, d = lax.axis_index("grp"), lax.axis_index("dev")
    me = g * N_DEV + d
    lane1 = iota((1, FD), 1)

    loads = [
        pltpu.make_async_copy(gap_hbm, gap_v, local_sem.at[0]),
        pltpu.make_async_copy(wgt_hbm, wgt_v, local_sem.at[1]),
        pltpu.make_async_copy(links_hbm, links_v, local_sem.at[2]),
        pltpu.make_async_copy(lens_hbm, lens_v, local_sem.at[3]),
        pltpu.make_async_copy(map_hbm, map_v, local_sem.at[4]),
    ]
    loads += [
        pltpu.make_async_copy(coup_hbm.at[s], coup_v.at[pl.ds(KC * s, KC), :], local_sem.at[5 + s])
        for s in range(SUB)
    ]
    loads.append(pltpu.make_async_copy(coarse_hbm, coarse_v, local_sem.at[9]))
    loads += [
        pltpu.make_async_copy(
            schur_hbm.at[s], schur_v.at[pl.ds(768 * s, 768), :], local_sem.at[10 + s]
        )
        for s in range(SUB)
    ]

    barrier = pltpu.get_barrier_semaphore()

    def offsets(i):
        return far_first(i // 4, 8), far_first(lax.rem(i, 4), 4)

    def slab_target(i):
        dz, dy = offsets(i)
        return lax.rem(d // 4 + dz, 8) * 4 + lax.rem(lax.rem(d, 4) + dy, 4)

    def slab_source(i):
        dz, dy = offsets(i)
        return lax.rem(d // 4 + 8 - dz, 8) * 4 + lax.rem(lax.rem(d, 4) + 4 - dy, 4)

    def each(axis, first, last, act):
        def body(i, c):
            if axis == "dev":
                act(slab_target(i), i)
            else:
                act(lax.rem(g + far_first(i, N_GRP), N_GRP), i)
            return c

        lax.fori_loop(first, last, body, 0)

    def greet(axis, n):
        def act(t, i):
            pl.semaphore_signal(barrier, inc=1, device_id={axis: t}, device_id_type=MESH)

        each(axis, 0, n - 1, act)

    own_rows = pl.ds(pl.multiple_of(4 * d, 4), 4)
    for buf in [fields0.at[i] for i in range(2)] + [fields.at[i] for i in range(ITERS)]:
        buf[own_rows, :] = jnp.zeros((4, FD), F32)
    meta[32:128, :] = jnp.zeros((96, FD), F32)
    slots[32:128, :] = jnp.zeros((96, FD), F32)
    greet("dev", N_DEV)
    greet("grp", N_GRP)
    for load in loads:
        load.start()

    def send(src, dst, sem, axis, t):
        pltpu.make_async_remote_copy(
            src_ref=src, dst_ref=dst, send_sem=send_sem.at[sem], recv_sem=recv_sem.at[sem],
            device_id={axis: t}, device_id_type=MESH,
        ).start()

    def send_all(axis, n, src_of, dst, sem):
        each(axis, 0, n - 1, lambda t, i: send(src_of(t), dst, sem, axis, t))

    def send_everywhere(src, sem):
        near = sorted(
            ((y, x, c) for y in range(4) for x in range(4) for c in range(2)),
            key=lambda o: -(min(o[0], 4 - o[0]) + min(o[1], 4 - o[1])),
        )

        def to_layer(z, places):
            for y, x, c in places:
                to_g = lax.rem(g // 2 + x, 4) * 2 + lax.rem(g + c, 2)
                to_d = z * 4 + lax.rem(lax.rem(d, 4) + y, 4)
                pltpu.make_async_remote_copy(
                    src_ref=src, dst_ref=src, send_sem=send_sem.at[sem], recv_sem=recv_sem.at[sem],
                    device_id=(to_g, to_d), device_id_type=MESH,
                ).start()

        def layer(i, c):
            to_layer(lax.rem(d // 4 + far_first(i, 8), 8), near)
            return c

        lax.fori_loop(0, 7, layer, 0)
        to_layer(d // 4, [o for o in near if o != (0, 0, 0)])

    acc_v[...] = jnp.zeros_like(acc_v)
    tmp[...] = jnp.zeros_like(tmp)
    tmp2[...] = jnp.zeros_like(tmp2)

    for load in loads[:5]:
        load.wait()
    links = links_v[...].astype(F32)
    tmp[0:SUB, 0:KC] = map_v[...].astype(F32)
    tmp2[0:SUB, 0:4] = links
    map_rows, link_rows = tmp[...], tmp2[...]
    meta_row = jnp.zeros((1, FD), F32)
    for s in range(SUB):
        meta_row += pltpu.roll(map_rows, KC * s, 1)[s : s + 1] if s else map_rows[0:1]
        meta_row += pltpu.roll(link_rows, CK + 4 * s, 1)[s : s + 1]
    meta[pl.ds(d, 1), :] = meta_row

    plus_dev = jnp.floor(links[0:1, 0:1] * 0.25)
    to_plus = (iota((N_DEV * SUB, FD), 0) // SUB).astype(F32) == plus_dev

    def chosen(values):
        first = jnp.concatenate([values[8:12]] * 32, axis=0)
        second = jnp.concatenate([values[12:16]] * 32, axis=0)
        return jnp.where(to_plus, first, second)

    own0 = []
    for i, src in enumerate((gap_v, wgt_v)):
        for f in range(FACES):
            fields0[i, 128 + 4 * f : 132 + 4 * f, :] = src[:, FD * f : FD * (f + 1)]
        values = fields0[i, 128:152, :]
        own0.append(values)
        sent0[i] = chosen(values)

    up, down = lax.rem(g + 1, N_GRP), lax.rem(g + N_GRP - 1, N_GRP)
    pl.semaphore_wait(barrier, N_DEV + N_GRP - 2)

    def send_fields(buf, out, sem):
        send_all(
            "dev", N_DEV,
            lambda t: out.at[pl.ds(pl.multiple_of(4 * t, 4), 4), :],
            buf.at[pl.ds(pl.multiple_of(4 * d, 4), 4), :], sem,
        )
        send(buf.at[pl.ds(132, 4), :], buf.at[pl.ds(152, 4), :], sem, "grp", down)
        send(buf.at[pl.ds(128, 4), :], buf.at[pl.ds(156, 4), :], sem, "grp", up)

    def await_fields(buf, sems, sem):
        await_bytes(buf.at[pl.ds(0, 4 * (N_DEV + 1)), :], sems.at[sem])

    S_F0, S_META, S_TA, S_TB, S_CX, S_F, S_R1, S_R2, S_R3, S_NEAR = (
        0, 2, 3, 4, 5, 6, 9, 12, 15, 18
    )

    for i in range(2):
        send_fields(fields0.at[i], sent0.at[i], S_F0 + i)
    own_meta = meta.at[pl.ds(d, 1), :]
    send_all("dev", N_DEV, lambda t: own_meta, own_meta, S_META)
    send(own_meta, meta.at[pl.ds(32, 1), :], S_META, "grp", down)
    send(own_meta, meta.at[pl.ds(33, 1), :], S_META, "grp", up)
    for load in loads[5:9]:
        load.wait()
    for j in range(PIECES):
        @pl.when(d != j)
        def _():
            send(
                coup_v.at[pl.ds(8 * (j % 12), 8), pl.ds(FD * (2 + j // 12), FD)],
                tiles_a.at[pl.ds(pl.multiple_of(8 * d, 8), 8), :], S_TA, "dev", j,
            )
    send(coup_v.at[:, pl.ds(FD, FD)], coup_x.at[0], S_CX, "grp", down)
    send(coup_v.at[:, pl.ds(0, FD)], coup_x.at[1], S_CX, "grp", up)

    row24 = iota((ROWS, FD), 0)
    row_of_lane = jnp.where(
        iota((ROWS, ROWS * FD), 1) // FD == iota((ROWS, ROWS * FD), 0), 1.0, 0.0
    ).astype(BF16)
    sign = (1 - 2 * (lax.rem(row24 // 4, 2))).astype(F32)
    sign_mask[0:8, :] = sign[0:8]
    lens = lens_v[...]
    for k in range(4):
        live = iota((SUB, FD), 1) < lens[:, k : k + 1]
        sign_mask[8 + 4 * k : 12 + 4 * k, :] = jnp.where(live, 1.0 - 2.0 * (k % 2), 0.0)
    jump_sign = sign_mask[...]
    slot = iota((SUB, FD), 0).astype(F32)
    slot_of = links - 4.0 * jnp.floor(links * 0.25)
    ones4 = jnp.ones((SUB, FD), F32)
    target[0:4, :] = slot + 152.0
    target[4:8, :] = slot + 156.0
    target[8:12, :] = ones4 * links[:, 0:1]
    target[12:16, :] = ones4 * links[:, 1:2]
    target[16:20, :] = ones4 * (slot_of[:, 2:3] + 148.0)
    target[20:24, :] = ones4 * (slot_of[:, 3:4] + 144.0)
    targets = target[...][:, 0:1]
    opposite_hot = jnp.where(targets == iota((ROWS, 160), 1).astype(F32), 1.0, 0.0).astype(BF16)

    loads[9].wait()
    coarse_p[...] = jnp.zeros_like(coarse_p)
    for j in range(HI):
        coarse_p[:, FD * j : FD * j + LO] = coarse_v[:, LO * j : LO * (j + 1)]
    for f in range(FACES):
        for s in range(SUB):
            r = f * SUB + s
            own_w[f, KC * s : KC * (s + 1), :] = (
                coup_v[KC * s : KC * (s + 1), FD * f : FD * (f + 1)] * jump_sign[r : r + 1]
            )

    for i in range(2):
        await_fields(fields0.at[i], recv_sem, S_F0 + i)
    residual = jump_sign * (own0[0] - pick_rows(opposite_hot, fields0[0]))
    scaling = own0[1] + pick_rows(opposite_hot, fields0[1])
    scaled = scaling * residual
    result = jnp.zeros_like(residual)
    direction = image_dir = local_dir = None
    coarse_dir = norm_before = curve_before = None

    def scattered(loads_of, first, last):
        parts = [part.astype(F32) for part in split(loads_of[first:last, :], 2)]
        for j in range(first, last):
            for q in range(2):
                placed[HI * q : HI * (q + 1), FD * j : FD * (j + 1)] = (
                    high_mask[:, FD * j : FD * (j + 1)] * parts[q][j - first : j - first + 1]
                ).astype(BF16)
        return dot(placed[:, FD * first : FD * last], low_hot[FD * first : FD * last, :])

    def sends_done(it):
        if it < 0:
            for i in range(2):
                await_fields(fields0.at[i], send_sem, S_F0 + i)
            await_bytes(meta.at[pl.ds(0, N_DEV + 1), :], send_sem.at[S_META])

            @pl.when(d < PIECES)
            def _():
                await_bytes(tiles_a.at[pl.ds(0, 8 * (PIECES - 1)), :], send_sem.at[S_TA])

            @pl.when(d >= PIECES)
            def _():
                await_bytes(tiles_a.at[pl.ds(0, 8 * PIECES), :], send_sem.at[S_TA])

            await_bytes(coup_x, send_sem.at[S_CX])
            return
        if it == 0:
            @pl.when(d < PIECES)
            def _():
                await_bytes(tiles_b.at[pl.ds(0, 8 * (N_DEV - 1)), :], send_sem.at[S_TB])

        await_fields(fields.at[it], send_sem, S_F + it)
        one = round1.at[it]
        await_bytes(one.at[pl.ds(0, FAR), :], send_sem.at[S_R1 + it])
        await_bytes(one.at[pl.ds(0, N_DEV - 1 - FAR), :], send_sem.at[S_NEAR + it])
        await_bytes(round2.at[it].at[pl.ds(0, N_DEV * N_GRP - 1), :], send_sem.at[S_R2 + it])
        await_bytes(round3.at[it].at[pl.ds(0, HI * (N_GRP - 1)), :], send_sem.at[S_R3 + it])

    for it in range(ITERS):
        load_now = sign * scaled
        for s in range(SUB):
            part = jnp.zeros((KC, FD), F32)
            for f in range(FACES):
                r = f * SUB + s
                part += coup_v[KC * s : KC * (s + 1), FD * f : FD * (f + 1)] * load_now[r : r + 1]
            acc_v[KC * s : KC * (s + 1), :] = part
        r1, rows_of_all, rhs_of_all = round1.at[it], round2.at[it], round3.at[it]
        r1[N_DEV - 1 :, :] = lane_sums(acc_v[...])
        own = r1.at[pl.ds(N_DEV - 1, 1), :]
        each("dev", 0, FAR, lambda t, i: send(own, r1.at[pl.ds(i, 1), :], S_R1 + it, "dev", t))
        each(
            "dev", FAR, N_DEV - 1,
            lambda t, i: send(own, r1.at[pl.ds(i, 1), :], S_NEAR + it, "dev", t),
        )

        if it == 0:
            for load in loads[10:]:
                load.wait()
        for s in range(SUB):
            rows_of_load = [load_now[h * SUB + s : h * SUB + s + 1] for h in range(FACES)]

            def block(f, c):
                rows = pl.ds(pl.multiple_of(768 * s + FD * f, FD), FD)
                part = schur_v[rows, 0:FD] * rows_of_load[0]
                for h in range(1, FACES):
                    part += schur_v[rows, FD * h : FD * (h + 1)] * rows_of_load[h]
                products[:, pl.ds(pl.multiple_of(FD * (f * SUB + s), FD), FD)] = part
                return c

            lax.fori_loop(0, FACES, block, 0)
        response = sum(dot_nt(row_of_lane, part) for part in split(products[...], 2))
        buf, out = fields.at[it], sent.at[it]
        buf[128:152, :] = response
        out[...] = chosen(response)
        send_fields(buf, out, S_F + it)
        norm_part = 0.5 * total(residual * scaled)
        curve_part = total(load_now * response)
        cross_part = None
        if it:
            cross_part = total(load_now * local_dir + sign * direction * response)

        if it == 0:
            await_bytes(meta.at[pl.ds(0, N_DEV + 1), :], recv_sem.at[S_META])
            table = meta[...]

            def reorder(i, c):
                slots[pl.ds(i, 1), :] = meta[pl.ds(slab_source(i), 1), :]
                return c

            lax.fori_loop(0, N_DEV, reorder, 0)
            ordered = slots[...]
            high = jnp.floor((ordered + 0.5) * (1.0 / LO))
            low = (ordered - LO * high).T
            hi_rows = iota((HI, FD), 0).astype(F32)
            lo_lanes = iota((FD, FD), 1).astype(F32)
            for j in range(N_DEV):
                cols = slice(FD * j, FD * (j + 1))
                high_mask[:, cols] = jnp.where(hi_rows == high[j : j + 1], 1.0, 0.0)
                low_hot[cols, :] = jnp.where(lo_lanes == low[:, j : j + 1], 1.0, 0.0).astype(BF16)

            @pl.when(d < PIECES)
            def _():
                tiles_a[pl.ds(pl.multiple_of(8 * d, 8), 8), :] = coup_v[
                    pl.ds(pl.multiple_of(8 * lax.rem(d, 12), 8), 8),
                    pl.ds(pl.multiple_of(FD * (2 + d // 12), FD), FD),
                ]
                await_bytes(tiles_a.at[pl.ds(0, 8 * (N_DEV - 1)), :], recv_sem.at[S_TA])
                spread = jnp.where(
                    iota((256, FD), 0) // 8 == iota((256, FD), 1), 1.0, 0.0
                ).astype(BF16)
                wanted = dot(spread, table.astype(BF16))
                which = CK + 1 - d // 12
                source = jnp.sum(
                    jnp.where(iota((256, FD), 1) == which, wanted, 0.0), axis=1, keepdims=True
                )
                source = 8.0 * jnp.floor(source * 0.25) + lax.rem(
                    iota((256, 1), 0), 8
                ).astype(F32)
                hot = jnp.where(iota((256, 256), 1).astype(F32) == source, 1.0, 0.0).astype(BF16)
                tiles_b[...] = pick_rows(hot, tiles_a[...])
                here = pl.ds(pl.multiple_of(8 * d, 8), 8)
                coup_a[here, :] = tiles_b[here, :]
                send_all(
                    "dev", N_DEV,
                    lambda t: tiles_b.at[pl.ds(pl.multiple_of(8 * t, 8), 8), :],
                    coup_a.at[here, :], S_TB,
                )

        sends_done(it - 1)

        await_bytes(r1.at[pl.ds(FAR, N_DEV - 1 - FAR), :], recv_sem.at[S_NEAR + it])
        summed = scattered(r1, FAR, N_DEV)
        await_bytes(r1.at[pl.ds(0, FAR), :], recv_sem.at[S_R1 + it])
        summed += scattered(r1, 0, FAR)
        slab_rhs = summed[0:HI] + summed[HI:]
        part = jnp.zeros((CK, FD), F32)
        for j in range(HI):
            part += coarse_p[:, FD * j : FD * (j + 1)] * slab_rhs[j : j + 1]
        acc_v[0:CK, :] = part
        row = lane_sums(acc_v[...])
        row = jnp.where(lane1 == LO, norm_part, row)
        row = jnp.where(lane1 == LO + 1, curve_part, row)
        if it:
            row = jnp.where(lane1 == LO + 2, cross_part, row)
        rows_of_all[pl.ds(me, 1), :] = row
        mine = rows_of_all.at[pl.ds(me, 1), :]
        send_everywhere(mine, S_R2 + it)
        here = pl.ds(pl.multiple_of(HI * g, HI), HI)
        rhs_of_all[here, :] = slab_rhs
        own_rhs = rhs_of_all.at[here, :]
        send_all("grp", N_GRP, lambda t: own_rhs, own_rhs, S_R3 + it)

        if it == 0:
            columns = table.T[0:CK]
            lane_f = iota((CK, FD), 1).astype(F32)

            def column(device):
                return jnp.sum(jnp.where(lane_f == device, columns, 0.0), axis=1, keepdims=True)

            def permuted(values, k):
                groups = []
                for s in range(SUB):
                    got = jnp.zeros((KC, FD), F32)
                    for j in range(SUB):
                        same = slot_of[s : s + 1, k : k + 1] == float(j)
                        got = jnp.where(same, values[KC * j : KC * (j + 1)], got)
                    groups.append(got)
                return jnp.concatenate(groups, axis=0)

            wide = jnp.zeros((CK, FD), F32)
            own_map = column(d.astype(F32)) + wide
            minus_dev = jnp.floor(links[0:1, 1:2] * 0.25)
            maps = [
                own_map,
                column(32.0) + wide,
                column(33.0) + wide,
                permuted(column(plus_dev) + wide, 0),
                permuted(column(minus_dev) + wide, 1),
                permuted(own_map, 2),
                permuted(own_map, 3),
            ]
            for i, m in enumerate(maps):
                high = jnp.floor((m + 0.5) * (1.0 / LO))
                rows = slice(CK * i, CK * (i + 1))
                gather_hi[rows, :] = jnp.where(high == lane_f, 1.0, 0.0).astype(BF16)
                gather_lo[rows, :] = jnp.where(m - LO * high == lane_f, 1.0, 0.0)

        await_fields(buf, recv_sem, S_F + it)
        local_jump = jump_sign * (response - pick_rows(opposite_hot, buf[...]))
        if it == 0:
            @pl.when(d < PIECES)
            def _():
                await_bytes(coup_a.at[pl.ds(0, 8 * (PIECES - 1)), :], recv_sem.at[S_TB])

            @pl.when(d >= PIECES)
            def _():
                await_bytes(coup_a.at[pl.ds(0, 8 * PIECES), :], recv_sem.at[S_TB])

            await_bytes(coup_x, recv_sem.at[S_CX])
            beyond = [
                coup_x[0],
                coup_x[1],
                permuted(coup_a[CK : 2 * CK, :], 0),
                permuted(coup_a[0:CK, :], 1),
                permuted(coup_v[:, FD * 5 : FD * 6], 2),
                permuted(coup_v[:, FD * 4 : FD * 5], 3),
            ]
            for f in range(FACES):
                for s in range(SUB):
                    r = f * SUB + s
                    next_w[f, KC * s : KC * (s + 1), :] = (
                        -jump_sign[r : r + 1] * beyond[f][KC * s : KC * (s + 1)]
                    )

        await_bytes(rhs_of_all.at[pl.ds(0, HI * (N_GRP - 1)), :], recv_sem.at[S_R3 + it])
        coarse_rhs = rhs_of_all[0:HI, :]
        for k in range(1, N_GRP):
            coarse_rhs += rhs_of_all[HI * k : HI * (k + 1), :]
        await_bytes(rows_of_all.at[pl.ds(0, N_DEV * N_GRP - 1), :], recv_sem.at[S_R2 + it])
        coarse_sol = rows_of_all[0:N_DEV, :]
        for k in range(1, N_GRP):
            coarse_sol += rows_of_all[N_DEV * k : N_DEV * (k + 1), :]
        sums = jnp.sum(coarse_sol, axis=0, keepdims=True)
        norm_now = sums[:, LO : LO + 1]
        curve = sums[:, LO + 1 : LO + 2] + total(coarse_sol * coarse_rhs)
        padded = jnp.concatenate([coarse_sol, jnp.zeros((FD - HI, FD), F32)], axis=0)
        at_corner = []
        sol_parts = split(padded, 2)
        for i in range(7):
            rows = slice(CK * i, CK * (i + 1))
            hot = gather_hi[rows, :]
            got = sum(dot(hot, p) for p in sol_parts) * gather_lo[rows, :]
            at_corner.append(jnp.sum(got, axis=1, keepdims=True))
        for f in range(FACES):
            both = own_w[f] * at_corner[0] + next_w[f] * at_corner[1 + f]
            for s in range(SUB):
                r = f * SUB + s
                target[r : r + 1, :] = jnp.sum(
                    both[KC * s : KC * (s + 1)], axis=0, keepdims=True
                )
        image = local_jump + target[...]

        if it == 0:
            direction, image_dir, local_dir, coarse_dir = scaled, image, response, coarse_rhs
        else:
            ratio = norm_now / norm_before
            cross = sums[:, LO + 2 : LO + 3] + 2.0 * total(coarse_sol * coarse_dir)
            curve = curve + ratio * cross + ratio * ratio * curve_before
            direction = scaled + ratio * direction
            image_dir = image + ratio * image_dir
            local_dir = response + ratio * local_dir
            coarse_dir = coarse_rhs + ratio * coarse_dir
        step = norm_now / curve
        norm_before, curve_before = norm_now, curve
        result = result + step * direction
        residual = residual - step * image_dir
        scaled = scaling * residual

    for f in range(FACES):
        out_ref[0, :, FD * f : FD * (f + 1)] = result[4 * f : 4 * f + 4]
        out_ref[1, :, FD * f : FD * (f + 1)] = residual[4 * f : 4 * f + 4]

    sends_done(ITERS - 1)


def per_device(*args):
    vmem = lambda *shape: pltpu.VMEM(shape, F32)
    field = jax.ShapeDtypeStruct((2, SUB, FACES * FD), F32)
    both = pl.pallas_call(
        kernel,
        out_shape=field,
        in_specs=[pl.BlockSpec(memory_space=pltpu.HBM)] * 8,
        out_specs=pl.BlockSpec(memory_space=pltpu.VMEM),
        scratch_shapes=[
            vmem(SUB, 768), vmem(SUB, 768),
            pltpu.VMEM((SUB, 4), jnp.int32), pltpu.VMEM((SUB, 4), jnp.int32),
            pltpu.VMEM((SUB, KC), jnp.int32),
            vmem(SUB * 768, 768), vmem(CK, 768), vmem(CK, 3072), vmem(CK, HI * FD),
            vmem(2, 160, FD), vmem(2, 128, FD),
            vmem(ITERS, 160, FD), vmem(ITERS, 128, FD),
            vmem(ROWS, FD), vmem(ROWS, FD), vmem(8, FD), vmem(8, FD),
            vmem(FD, FD), vmem(FD, FD), vmem(256, FD), vmem(256, FD), vmem(2 * CK, FD), vmem(2, CK, FD),
            vmem(FACES, CK, FD), vmem(FACES, CK, FD),
            vmem(HI, HI * FD), pltpu.VMEM((HI * FD, FD), BF16),
            pltpu.VMEM((7 * CK, FD), BF16), vmem(7 * CK, FD), vmem(FD, FD), vmem(FD, ROWS * FD), pltpu.VMEM((2 * HI, HI * FD), BF16),
            vmem(ITERS, N_DEV, FD), vmem(ITERS, N_DEV * N_GRP, FD), vmem(ITERS, HI * N_GRP, FD),
            pltpu.SemaphoreType.DMA((14,)),
            pltpu.SemaphoreType.DMA((21,)),
            pltpu.SemaphoreType.DMA((21,)),
        ],
        compiler_params=pltpu.CompilerParams(
            collective_id=0, has_side_effects=True, vmem_limit_bytes=63 * 1024 * 1024
        ),
    )(*args)
    return both[0], both[1]


def solution(mesh):
    return jax.shard_map(
        per_device,
        mesh=mesh,
        in_specs=(
            P(("grp", "dev"), None),
            P(("grp", "dev"), None),
            P("dev", None),
            P("dev", None),
            P(("grp", "dev"), None, None),
            P(("grp", "dev"), None),
            P(("grp", "dev"), None, None),
            P("dev", None),
        ),
        out_specs=(P(("grp", "dev"), None), P(("grp", "dev"), None)),
        check_vma=False,
    )
```

```python
import functools

import jax
import jax.numpy as jnp
from jax import lax
from jax.experimental import pallas as pl
from jax.experimental.pallas import tpu as pltpu
from jax.sharding import PartitionSpec as P

ITERS = 3
MESH = pl.DeviceIdType.MESH
F32 = jnp.float32
BF16 = jnp.bfloat16
N_GRP, N_DEV = 8, 32
SUB, KC, FD, FACES = 4, 24, 128, 6
ROWS = SUB * FACES
CK = SUB * KC
HI, LO = 32, 96
FAR = 8
PIECES = 2 * CK // 8


def iota(shape, dim):
    return lax.broadcasted_iota(jnp.int32, shape, dim)


def split(x, parts):
    out = []
    for _ in range(parts - 1):
        top = x.astype(BF16)
        out.append(top)
        x = x - top.astype(F32)
    out.append(x.astype(BF16))
    return out


def dot(a, b):
    return jnp.dot(a, b, preferred_element_type=F32)


def dot_nt(a, b):
    return lax.dot_general(a, b, (((1,), (1,)), ((), ())), preferred_element_type=F32)


def pick_rows(one_hot, x):
    return sum(dot(one_hot, part) for part in split(x, 2))


def lane_sums(x):
    ones = jnp.ones((8, 2 * x.shape[1]), BF16)
    return dot_nt(ones, jnp.concatenate(split(x, 2), axis=1))[0:1]


def total(x):
    return jnp.sum(jnp.sum(x, axis=0, keepdims=True), axis=1, keepdims=True)


def await_bytes(ref, sem):
    pltpu.make_async_copy(ref, ref, sem).wait()


def far_first(i, n):
    return n // 2 + (1 - 2 * lax.rem(i, 2)) * ((i + 1) // 2)


def kernel(
    gap_hbm, wgt_hbm, links_hbm, lens_hbm, schur_hbm, map_hbm, coup_hbm, coarse_hbm,
    out_ref,
    gap_v, wgt_v, links_v, lens_v, map_v, schur_v, coup_v, coarse_v, coarse_p,
    fields0, sent0, fields, sent, target, sign_mask, tmp, tmp2,
    meta, slots, tiles_a, tiles_b, coup_a, coup_x, own_w, next_w,
    high_mask, low_hot, gather_hi, gather_lo, acc_v, products, placed,
    round1, round2, round3,
    local_sem, send_sem, recv_sem,
):
    g, d = lax.axis_index("grp"), lax.axis_index("dev")
    me = g * N_DEV + d
    lane1 = iota((1, FD), 1)

    loads = [
        pltpu.make_async_copy(gap_hbm, gap_v, local_sem.at[0]),
        pltpu.make_async_copy(wgt_hbm, wgt_v, local_sem.at[1]),
        pltpu.make_async_copy(links_hbm, links_v, local_sem.at[2]),
        pltpu.make_async_copy(lens_hbm, lens_v, local_sem.at[3]),
        pltpu.make_async_copy(map_hbm, map_v, local_sem.at[4]),
    ]
    loads += [
        pltpu.make_async_copy(coup_hbm.at[s], coup_v.at[pl.ds(KC * s, KC), :], local_sem.at[5 + s])
        for s in range(SUB)
    ]
    loads.append(pltpu.make_async_copy(coarse_hbm, coarse_v, local_sem.at[9]))
    loads += [
        pltpu.make_async_copy(
            schur_hbm.at[s], schur_v.at[pl.ds(768 * s, 768), :], local_sem.at[10 + s]
        )
        for s in range(SUB)
    ]

    barrier = pltpu.get_barrier_semaphore()

    def offsets(i):
        return far_first(i // 4, 8), far_first(lax.rem(i, 4), 4)

    def slab_target(i):
        dz, dy = offsets(i)
        return lax.rem(d // 4 + dz, 8) * 4 + lax.rem(lax.rem(d, 4) + dy, 4)

    def slab_source(i):
        dz, dy = offsets(i)
        return lax.rem(d // 4 + 8 - dz, 8) * 4 + lax.rem(lax.rem(d, 4) + 4 - dy, 4)

    def each(axis, first, last, act):
        def body(i, c):
            if axis == "dev":
                act(slab_target(i), i)
            else:
                act(lax.rem(g + far_first(i, N_GRP), N_GRP), i)
            return c

        lax.fori_loop(first, last, body, 0)

    def greet(axis, n):
        def act(t, i):
            pl.semaphore_signal(barrier, inc=1, device_id={axis: t}, device_id_type=MESH)

        each(axis, 0, n - 1, act)

    own_rows = pl.ds(pl.multiple_of(4 * d, 4), 4)
    for buf in [fields0.at[i] for i in range(2)] + [fields.at[i] for i in range(ITERS)]:
        buf[own_rows, :] = jnp.zeros((4, FD), F32)
    meta[32:128, :] = jnp.zeros((96, FD), F32)
    slots[32:128, :] = jnp.zeros((96, FD), F32)
    greet("dev", N_DEV)
    greet("grp", N_GRP)
    for load in loads:
        load.start()

    def send(src, dst, sem, axis, t):
        pltpu.make_async_remote_copy(
            src_ref=src, dst_ref=dst, send_sem=send_sem.at[sem], recv_sem=recv_sem.at[sem],
            device_id={axis: t}, device_id_type=MESH,
        ).start()

    def send_all(axis, n, src_of, dst, sem):
        each(axis, 0, n - 1, lambda t, i: send(src_of(t), dst, sem, axis, t))

    def send_everywhere(src, sem):
        near = sorted(
            ((y, x, c) for y in range(4) for x in range(4) for c in range(2)),
            key=lambda o: -(min(o[0], 4 - o[0]) + min(o[1], 4 - o[1])),
        )

        def to_layer(z, places):
            for y, x, c in places:
                to_g = lax.rem(g // 2 + x, 4) * 2 + lax.rem(g + c, 2)
                to_d = z * 4 + lax.rem(lax.rem(d, 4) + y, 4)
                pltpu.make_async_remote_copy(
                    src_ref=src, dst_ref=src, send_sem=send_sem.at[sem], recv_sem=recv_sem.at[sem],
                    device_id=(to_g, to_d), device_id_type=MESH,
                ).start()

        def layer(i, c):
            to_layer(lax.rem(d // 4 + far_first(i, 8), 8), near)
            return c

        lax.fori_loop(0, 7, layer, 0)
        to_layer(d // 4, [o for o in near if o != (0, 0, 0)])

    acc_v[...] = jnp.zeros_like(acc_v)
    tmp[...] = jnp.zeros_like(tmp)
    tmp2[...] = jnp.zeros_like(tmp2)

    for load in loads[:5]:
        load.wait()
    links = links_v[...].astype(F32)
    tmp[0:SUB, 0:KC] = map_v[...].astype(F32)
    tmp2[0:SUB, 0:4] = links
    map_rows, link_rows = tmp[...], tmp2[...]
    meta_row = jnp.zeros((1, FD), F32)
    for s in range(SUB):
        meta_row += pltpu.roll(map_rows, KC * s, 1)[s : s + 1] if s else map_rows[0:1]
        meta_row += pltpu.roll(link_rows, CK + 4 * s, 1)[s : s + 1]
    meta[pl.ds(d, 1), :] = meta_row

    plus_dev = jnp.floor(links[0:1, 0:1] * 0.25)
    to_plus = (iota((N_DEV * SUB, FD), 0) // SUB).astype(F32) == plus_dev

    def chosen(values):
        first = jnp.concatenate([values[8:12]] * 32, axis=0)
        second = jnp.concatenate([values[12:16]] * 32, axis=0)
        return jnp.where(to_plus, first, second)

    own0 = []
    for i, src in enumerate((gap_v, wgt_v)):
        for f in range(FACES):
            fields0[i, 128 + 4 * f : 132 + 4 * f, :] = src[:, FD * f : FD * (f + 1)]
        values = fields0[i, 128:152, :]
        own0.append(values)
        sent0[i] = chosen(values)

    up, down = lax.rem(g + 1, N_GRP), lax.rem(g + N_GRP - 1, N_GRP)
    pl.semaphore_wait(barrier, N_DEV + N_GRP - 2)

    def send_fields(buf, out, sem):
        send_all(
            "dev", N_DEV,
            lambda t: out.at[pl.ds(pl.multiple_of(4 * t, 4), 4), :],
            buf.at[pl.ds(pl.multiple_of(4 * d, 4), 4), :], sem,
        )
        send(buf.at[pl.ds(132, 4), :], buf.at[pl.ds(152, 4), :], sem, "grp", down)
        send(buf.at[pl.ds(128, 4), :], buf.at[pl.ds(156, 4), :], sem, "grp", up)

    def await_fields(buf, sems, sem):
        await_bytes(buf.at[pl.ds(0, 4 * (N_DEV + 1)), :], sems.at[sem])

    S_F0, S_META, S_TA, S_TB, S_CX, S_F, S_R1, S_R2, S_R3, S_NEAR = (
        0, 2, 3, 4, 5, 6, 9, 12, 15, 18
    )

    for i in range(2):
        send_fields(fields0.at[i], sent0.at[i], S_F0 + i)
    own_meta = meta.at[pl.ds(d, 1), :]
    send_all("dev", N_DEV, lambda t: own_meta, own_meta, S_META)
    send(own_meta, meta.at[pl.ds(32, 1), :], S_META, "grp", down)
    send(own_meta, meta.at[pl.ds(33, 1), :], S_META, "grp", up)
    for load in loads[5:9]:
        load.wait()
    for j in range(PIECES):
        @pl.when(d != j)
        def _():
            send(
                coup_v.at[pl.ds(8 * (j % 12), 8), pl.ds(FD * (2 + j // 12), FD)],
                tiles_a.at[pl.ds(pl.multiple_of(8 * d, 8), 8), :], S_TA, "dev", j,
            )
    send(coup_v.at[:, pl.ds(FD, FD)], coup_x.at[0], S_CX, "grp", down)
    send(coup_v.at[:, pl.ds(0, FD)], coup_x.at[1], S_CX, "grp", up)

    row24 = iota((ROWS, FD), 0)
    row_of_lane = jnp.where(
        iota((ROWS, ROWS * FD), 1) // FD == iota((ROWS, ROWS * FD), 0), 1.0, 0.0
    ).astype(BF16)
    sign = (1 - 2 * (lax.rem(row24 // 4, 2))).astype(F32)
    sign_mask[0:8, :] = sign[0:8]
    lens = lens_v[...]
    for k in range(4):
        live = iota((SUB, FD), 1) < lens[:, k : k + 1]
        sign_mask[8 + 4 * k : 12 + 4 * k, :] = jnp.where(live, 1.0 - 2.0 * (k % 2), 0.0)
    jump_sign = sign_mask[...]
    slot = iota((SUB, FD), 0).astype(F32)
    slot_of = links - 4.0 * jnp.floor(links * 0.25)
    ones4 = jnp.ones((SUB, FD), F32)
    target[0:4, :] = slot + 152.0
    target[4:8, :] = slot + 156.0
    target[8:12, :] = ones4 * links[:, 0:1]
    target[12:16, :] = ones4 * links[:, 1:2]
    target[16:20, :] = ones4 * (slot_of[:, 2:3] + 148.0)
    target[20:24, :] = ones4 * (slot_of[:, 3:4] + 144.0)
    targets = target[...][:, 0:1]
    opposite_hot = jnp.where(targets == iota((ROWS, 160), 1).astype(F32), 1.0, 0.0).astype(BF16)

    loads[9].wait()
    coarse_p[...] = jnp.zeros_like(coarse_p)
    for j in range(HI):
        coarse_p[:, FD * j : FD * j + LO] = coarse_v[:, LO * j : LO * (j + 1)]
    for f in range(FACES):
        for s in range(SUB):
            r = f * SUB + s
            own_w[f, KC * s : KC * (s + 1), :] = (
                coup_v[KC * s : KC * (s + 1), FD * f : FD * (f + 1)] * jump_sign[r : r + 1]
            )

    for i in range(2):
        await_fields(fields0.at[i], recv_sem, S_F0 + i)
    residual = jump_sign * (own0[0] - pick_rows(opposite_hot, fields0[0]))
    scaling = own0[1] + pick_rows(opposite_hot, fields0[1])
    scaled = scaling * residual
    result = jnp.zeros_like(residual)
    direction = image_dir = local_dir = None
    coarse_dir = norm_before = curve_before = None

    def scattered(loads_of, first, last):
        parts = [part.astype(F32) for part in split(loads_of[first:last, :], 2)]
        for j in range(first, last):
            for q in range(2):
                placed[HI * q : HI * (q + 1), FD * j : FD * (j + 1)] = (
                    high_mask[:, FD * j : FD * (j + 1)] * parts[q][j - first : j - first + 1]
                ).astype(BF16)
        return dot(placed[:, FD * first : FD * last], low_hot[FD * first : FD * last, :])

    def sends_done(it):
        if it < 0:
            for i in range(2):
                await_fields(fields0.at[i], send_sem, S_F0 + i)
            await_bytes(meta.at[pl.ds(0, N_DEV + 1), :], send_sem.at[S_META])

            @pl.when(d < PIECES)
            def _():
                await_bytes(tiles_a.at[pl.ds(0, 8 * (PIECES - 1)), :], send_sem.at[S_TA])

            @pl.when(d >= PIECES)
            def _():
                await_bytes(tiles_a.at[pl.ds(0, 8 * PIECES), :], send_sem.at[S_TA])

            await_bytes(coup_x, send_sem.at[S_CX])
            return
        if it == 0:
            @pl.when(d < PIECES)
            def _():
                await_bytes(tiles_b.at[pl.ds(0, 8 * (N_DEV - 1)), :], send_sem.at[S_TB])

        await_fields(fields.at[it], send_sem, S_F + it)
        one = round1.at[it]
        await_bytes(one.at[pl.ds(0, FAR), :], send_sem.at[S_R1 + it])
        await_bytes(one.at[pl.ds(0, N_DEV - 1 - FAR), :], send_sem.at[S_NEAR + it])
        await_bytes(round2.at[it].at[pl.ds(0, N_DEV * N_GRP - 1), :], send_sem.at[S_R2 + it])
        await_bytes(round3.at[it].at[pl.ds(0, HI * (N_GRP - 1)), :], send_sem.at[S_R3 + it])

    for it in range(ITERS):
        load_now = sign * scaled
        for s in range(SUB):
            part = jnp.zeros((KC, FD), F32)
            for f in range(FACES):
                r = f * SUB + s
                part += coup_v[KC * s : KC * (s + 1), FD * f : FD * (f + 1)] * load_now[r : r + 1]
            acc_v[KC * s : KC * (s + 1), :] = part
        r1, rows_of_all, rhs_of_all = round1.at[it], round2.at[it], round3.at[it]
        r1[N_DEV - 1 :, :] = lane_sums(acc_v[...])
        own = r1.at[pl.ds(N_DEV - 1, 1), :]
        each("dev", 0, FAR, lambda t, i: send(own, r1.at[pl.ds(i, 1), :], S_R1 + it, "dev", t))
        each(
            "dev", FAR, N_DEV - 1,
            lambda t, i: send(own, r1.at[pl.ds(i, 1), :], S_NEAR + it, "dev", t),
        )

        if it == 0:
            for load in loads[10:]:
                load.wait()
        for s in range(SUB):
            rows_of_load = [load_now[h * SUB + s : h * SUB + s + 1] for h in range(FACES)]

            def block(f, c):
                rows = pl.ds(pl.multiple_of(768 * s + FD * f, FD), FD)
                part = schur_v[rows, 0:FD] * rows_of_load[0]
                for h in range(1, FACES):
                    part += schur_v[rows, FD * h : FD * (h + 1)] * rows_of_load[h]
                products[:, pl.ds(pl.multiple_of(FD * (f * SUB + s), FD), FD)] = part
                return c

            lax.fori_loop(0, FACES, block, 0)
        response = sum(dot_nt(row_of_lane, part) for part in split(products[...], 2))
        buf, out = fields.at[it], sent.at[it]
        buf[128:152, :] = response
        out[...] = chosen(response)
        send_fields(buf, out, S_F + it)
        norm_part = 0.5 * total(residual * scaled)
        curve_part = total(load_now * response)
        cross_part = None
        if it:
            cross_part = total(load_now * local_dir + sign * direction * response)

        if it == 0:
            await_bytes(meta.at[pl.ds(0, N_DEV + 1), :], recv_sem.at[S_META])
            table = meta[...]

            def reorder(i, c):
                slots[pl.ds(i, 1), :] = meta[pl.ds(slab_source(i), 1), :]
                return c

            lax.fori_loop(0, N_DEV, reorder, 0)
            ordered = slots[...]
            high = jnp.floor((ordered + 0.5) * (1.0 / LO))
            low = (ordered - LO * high).T
            hi_rows = iota((HI, FD), 0).astype(F32)
            lo_lanes = iota((FD, FD), 1).astype(F32)
            for j in range(N_DEV):
                cols = slice(FD * j, FD * (j + 1))
                high_mask[:, cols] = jnp.where(hi_rows == high[j : j + 1], 1.0, 0.0)
                low_hot[cols, :] = jnp.where(lo_lanes == low[:, j : j + 1], 1.0, 0.0).astype(BF16)

            @pl.when(d < PIECES)
            def _():
                tiles_a[pl.ds(pl.multiple_of(8 * d, 8), 8), :] = coup_v[
                    pl.ds(pl.multiple_of(8 * lax.rem(d, 12), 8), 8),
                    pl.ds(pl.multiple_of(FD * (2 + d // 12), FD), FD),
                ]
                await_bytes(tiles_a.at[pl.ds(0, 8 * (N_DEV - 1)), :], recv_sem.at[S_TA])
                spread = jnp.where(
                    iota((256, FD), 0) // 8 == iota((256, FD), 1), 1.0, 0.0
                ).astype(BF16)
                wanted = dot(spread, table.astype(BF16))
                which = CK + 1 - d // 12
                source = jnp.sum(
                    jnp.where(iota((256, FD), 1) == which, wanted, 0.0), axis=1, keepdims=True
                )
                source = 8.0 * jnp.floor(source * 0.25) + lax.rem(
                    iota((256, 1), 0), 8
                ).astype(F32)
                hot = jnp.where(iota((256, 256), 1).astype(F32) == source, 1.0, 0.0).astype(BF16)
                tiles_b[...] = pick_rows(hot, tiles_a[...])
                here = pl.ds(pl.multiple_of(8 * d, 8), 8)
                coup_a[here, :] = tiles_b[here, :]
                send_all(
                    "dev", N_DEV,
                    lambda t: tiles_b.at[pl.ds(pl.multiple_of(8 * t, 8), 8), :],
                    coup_a.at[here, :], S_TB,
                )

        sends_done(it - 1)

        await_bytes(r1.at[pl.ds(FAR, N_DEV - 1 - FAR), :], recv_sem.at[S_NEAR + it])
        summed = scattered(r1, FAR, N_DEV)
        await_bytes(r1.at[pl.ds(0, FAR), :], recv_sem.at[S_R1 + it])
        summed += scattered(r1, 0, FAR)
        slab_rhs = summed[0:HI] + summed[HI:]
        part = jnp.zeros((CK, FD), F32)
        for j in range(HI):
            part += coarse_p[:, FD * j : FD * (j + 1)] * slab_rhs[j : j + 1]
        acc_v[0:CK, :] = part
        row = lane_sums(acc_v[...])
        row = jnp.where(lane1 == LO, norm_part, row)
        row = jnp.where(lane1 == LO + 1, curve_part, row)
        if it:
            row = jnp.where(lane1 == LO + 2, cross_part, row)
        rows_of_all[pl.ds(me, 1), :] = row
        mine = rows_of_all.at[pl.ds(me, 1), :]
        send_everywhere(mine, S_R2 + it)
        here = pl.ds(pl.multiple_of(HI * g, HI), HI)
        rhs_of_all[here, :] = slab_rhs
        own_rhs = rhs_of_all.at[here, :]
        send_all("grp", N_GRP, lambda t: own_rhs, own_rhs, S_R3 + it)

        if it == 0:
            columns = table.T[0:CK]
            lane_f = iota((CK, FD), 1).astype(F32)

            def column(device):
                return jnp.sum(jnp.where(lane_f == device, columns, 0.0), axis=1, keepdims=True)

            def permuted(values, k):
                groups = []
                for s in range(SUB):
                    got = jnp.zeros((KC, FD), F32)
                    for j in range(SUB):
                        same = slot_of[s : s + 1, k : k + 1] == float(j)
                        got = jnp.where(same, values[KC * j : KC * (j + 1)], got)
                    groups.append(got)
                return jnp.concatenate(groups, axis=0)

            wide = jnp.zeros((CK, FD), F32)
            own_map = column(d.astype(F32)) + wide
            minus_dev = jnp.floor(links[0:1, 1:2] * 0.25)
            maps = [
                own_map,
                column(32.0) + wide,
                column(33.0) + wide,
                permuted(column(plus_dev) + wide, 0),
                permuted(column(minus_dev) + wide, 1),
                permuted(own_map, 2),
                permuted(own_map, 3),
            ]
            for i, m in enumerate(maps):
                high = jnp.floor((m + 0.5) * (1.0 / LO))
                rows = slice(CK * i, CK * (i + 1))
                twice = (high == lane_f) | (high + HI == lane_f) | (high + 2 * HI == lane_f)
                gather_hi[rows, :] = jnp.where(twice, 1.0, 0.0).astype(BF16)
                gather_lo[rows, :] = jnp.where(m - LO * high == lane_f, 1.0, 0.0)

        await_fields(buf, recv_sem, S_F + it)
        local_jump = jump_sign * (response - pick_rows(opposite_hot, buf[...]))
        if it == 0:
            @pl.when(d < PIECES)
            def _():
                await_bytes(coup_a.at[pl.ds(0, 8 * (PIECES - 1)), :], recv_sem.at[S_TB])

            @pl.when(d >= PIECES)
            def _():
                await_bytes(coup_a.at[pl.ds(0, 8 * PIECES), :], recv_sem.at[S_TB])

            await_bytes(coup_x, recv_sem.at[S_CX])
            beyond = [
                coup_x[0],
                coup_x[1],
                permuted(coup_a[CK : 2 * CK, :], 0),
                permuted(coup_a[0:CK, :], 1),
                permuted(coup_v[:, FD * 5 : FD * 6], 2),
                permuted(coup_v[:, FD * 4 : FD * 5], 3),
            ]
            for f in range(FACES):
                for s in range(SUB):
                    r = f * SUB + s
                    next_w[f, KC * s : KC * (s + 1), :] = (
                        -jump_sign[r : r + 1] * beyond[f][KC * s : KC * (s + 1)]
                    )

        await_bytes(rhs_of_all.at[pl.ds(0, HI * (N_GRP - 1)), :], recv_sem.at[S_R3 + it])
        coarse_rhs = rhs_of_all[0:HI, :]
        for k in range(1, N_GRP):
            coarse_rhs += rhs_of_all[HI * k : HI * (k + 1), :]
        await_bytes(rows_of_all.at[pl.ds(0, N_DEV * N_GRP - 1), :], recv_sem.at[S_R2 + it])
        coarse_sol = rows_of_all[0:N_DEV, :]
        for k in range(1, N_GRP):
            coarse_sol += rows_of_all[N_DEV * k : N_DEV * (k + 1), :]
        sums = jnp.sum(coarse_sol, axis=0, keepdims=True)
        norm_now = sums[:, LO : LO + 1]
        curve = sums[:, LO + 1 : LO + 2] + total(coarse_sol * coarse_rhs)
        sol_parts = jnp.concatenate(
            split(coarse_sol, 3) + [jnp.zeros((FD - 3 * HI, FD), BF16)], axis=0
        )
        at_corner = []
        for i in range(7):
            rows = slice(CK * i, CK * (i + 1))
            got = dot(gather_hi[rows, :], sol_parts) * gather_lo[rows, :]
            at_corner.append(jnp.sum(got, axis=1, keepdims=True))
        for f in range(FACES):
            both = own_w[f] * at_corner[0] + next_w[f] * at_corner[1 + f]
            for s in range(SUB):
                r = f * SUB + s
                target[r : r + 1, :] = jnp.sum(
                    both[KC * s : KC * (s + 1)], axis=0, keepdims=True
                )
        image = local_jump + target[...]

        if it == 0:
            direction, image_dir, local_dir, coarse_dir = scaled, image, response, coarse_rhs
        else:
            ratio = norm_now / norm_before
            cross = sums[:, LO + 2 : LO + 3] + 2.0 * total(coarse_sol * coarse_dir)
            curve = curve + ratio * cross + ratio * ratio * curve_before
            direction = scaled + ratio * direction
            image_dir = image + ratio * image_dir
            local_dir = response + ratio * local_dir
            coarse_dir = coarse_rhs + ratio * coarse_dir
        step = norm_now / curve
        norm_before, curve_before = norm_now, curve
        result = result + step * direction
        residual = residual - step * image_dir
        scaled = scaling * residual

    for f in range(FACES):
        out_ref[0, :, FD * f : FD * (f + 1)] = result[4 * f : 4 * f + 4]
        out_ref[1, :, FD * f : FD * (f + 1)] = residual[4 * f : 4 * f + 4]

    sends_done(ITERS - 1)


def per_device(*args):
    vmem = lambda *shape: pltpu.VMEM(shape, F32)
    field = jax.ShapeDtypeStruct((2, SUB, FACES * FD), F32)
    both = pl.pallas_call(
        kernel,
        out_shape=field,
        in_specs=[pl.BlockSpec(memory_space=pltpu.HBM)] * 8,
        out_specs=pl.BlockSpec(memory_space=pltpu.VMEM),
        scratch_shapes=[
            vmem(SUB, 768), vmem(SUB, 768),
            pltpu.VMEM((SUB, 4), jnp.int32), pltpu.VMEM((SUB, 4), jnp.int32),
            pltpu.VMEM((SUB, KC), jnp.int32),
            vmem(SUB * 768, 768), vmem(CK, 768), vmem(CK, 3072), vmem(CK, HI * FD),
            vmem(2, 160, FD), vmem(2, 128, FD),
            vmem(ITERS, 160, FD), vmem(ITERS, 128, FD),
            vmem(ROWS, FD), vmem(ROWS, FD), vmem(8, FD), vmem(8, FD),
            vmem(FD, FD), vmem(FD, FD), vmem(256, FD), vmem(256, FD), vmem(2 * CK, FD), vmem(2, CK, FD),
            vmem(FACES, CK, FD), vmem(FACES, CK, FD),
            vmem(HI, HI * FD), pltpu.VMEM((HI * FD, FD), BF16),
            pltpu.VMEM((7 * CK, FD), BF16), vmem(7 * CK, FD), vmem(FD, FD), vmem(FD, ROWS * FD), pltpu.VMEM((2 * HI, HI * FD), BF16),
            vmem(ITERS, N_DEV, FD), vmem(ITERS, N_DEV * N_GRP, FD), vmem(ITERS, HI * N_GRP, FD),
            pltpu.SemaphoreType.DMA((14,)),
            pltpu.SemaphoreType.DMA((21,)),
            pltpu.SemaphoreType.DMA((21,)),
        ],
        compiler_params=pltpu.CompilerParams(
            collective_id=0, has_side_effects=True, vmem_limit_bytes=63 * 1024 * 1024
        ),
    )(*args)
    return both[0], both[1]


def solution(mesh):
    return jax.shard_map(
        per_device,
        mesh=mesh,
        in_specs=(
            P(("grp", "dev"), None),
            P(("grp", "dev"), None),
            P("dev", None),
            P("dev", None),
            P(("grp", "dev"), None, None),
            P(("grp", "dev"), None),
            P(("grp", "dev"), None, None),
            P("dev", None),
        ),
        out_specs=(P(("grp", "dev"), None), P(("grp", "dev"), None)),
        check_vma=False,
    )
```
